32 devices in a mesh: tile: 16 (over z, y, x), slide: 2 (over core).
Axes of the slice: x: 2, y: 2, z: 4, core: 2. Of those that a mesh axis runs over, the one named last changes fastest.
Arguments:
- features: bfloat16 [64, 32, 32, 256], P(('slide', 'tile')), parts along dimension 0, may hold values from -8 to 8
- neighbours: int32 [64, 8], P(('slide', 'tile')), parts along dimension 0, may hold values from 0 to 32, as said below
- conv_weight: bfloat16 [3, 3, 256, 256], replicated, may hold values from -0.125 to 0.125
- patch_weight: bfloat16 [4096, 768], replicated, may hold values from -1 to 1
- query_weight: bfloat16 [768, 768], replicated, may hold values from -2 to 2
- key_weight: bfloat16 [768, 768], replicated, may hold values from -2 to 2
- value_weight: bfloat16 [768, 768], replicated, may hold values from -0.21875 to 0.21875
- output_weight: bfloat16 [768, 768], replicated, may hold values from -0.21875 to 0.21875
- cotangent: bfloat16 [4096, 768], P(('slide', 'tile')), parts along dimension 0, may hold values from -6 to 6
Outputs:
- mixed: bfloat16 [4096, 768], P(('slide', 'tile')), parts along dimension 0
- output_grad: float32 [1536, 768], P('slide'), parts along dimension 0
The draws below stay inside these ranges and needn't reach their ends.
There are 2 independent parts, one for each index of `slide`. The reference program is written for one: setup_inputs(seed, part) draws one part's arguments, and reference() takes and returns one part's arrays. A program takes and returns all parts, laid end to end along the dimension named above; an argument that names none is the same for every part. Nothing has to cross between parts.
Inputs may be any that keep to these rules, and one draw needn't show every extreme that they name: Tiles are tissue cells of a grid 16 cells wide; the tile numbers are given to the tissue cells in a drawn order, so neighbours may have any numbers; each entry is the index of the tissue tile at that grid offset, or 32.
All inputs are finite; a program needn't handle non-finite values.
Results may differ from the reference program's by a relative error of at most 0.02.
Values may be sent and summed in bfloat16 or wider, within the bound.
A program may use at most 192 MiB of HBM per device.

```python
import math
import jax
import jax.numpy as jnp
from jax import lax

CELLS = 32
CH = 256
PATCH = 4
HEADS = 12
HD = 64
DM = 768
TOK_DEV = 128
TILES = 32
TOKENS = 2048
N_TILE = 16


def draw_neighbours(key, part):
    cells = 2 * TILES
    order = jax.random.permutation(key, cells)
    chosen = jnp.sort(order[:TILES])
    numbering = jax.random.permutation(jax.random.fold_in(key, 5), TILES)
    cell_of = chosen[numbering]
    rows = cell_of // 16
    cols = cell_of % 16
    height = cells // 16
    grid_map = jnp.full((cells,), TILES, jnp.int32).at[cell_of].set(jnp.arange(TILES, dtype=jnp.int32))
    offsets = [(-1, -1), (-1, 0), (-1, 1), (0, -1), (0, 1), (1, -1), (1, 0), (1, 1)]
    result = []
    for row_off, col_off in offsets:
        near_row = rows + row_off
        near_col = cols + col_off
        inside = (near_row >= 0) & (near_row < height) & (near_col >= 0) & (near_col < 16)
        place = jnp.clip(near_row * 16 + near_col, 0, cells - 1)
        result.append(jnp.where(inside, grid_map[place], TILES))
    return jnp.stack(result, axis=1).astype(jnp.int32)


def bounded_normal(key, shape):
    return jnp.clip(jax.random.normal(key, shape, jnp.float32), -5.0, 5.0)


def shared_pattern(key):
    base = jax.random.fold_in(key, 9001)
    token_signs = (2 * jax.random.randint(jax.random.fold_in(base, 1), (DM,), 0, 2) - 1).astype(jnp.float32)
    chosen_head = jax.random.randint(jax.random.fold_in(base, 2), (), 0, HEADS)
    head_signs = (2 * jax.random.randint(jax.random.fold_in(base, 3), (DM,), 0, 2) - 1).astype(jnp.float32)
    inside = jnp.arange(DM) // HD == chosen_head
    head_dir = jnp.where(inside, head_signs, 0.0) / math.sqrt(HD)
    return (token_signs, head_dir)


def drawn_projection(key, salt):
    token_signs, head_dir = shared_pattern(key)
    drawn = bounded_normal(jax.random.fold_in(key, salt), (DM, DM)) / math.sqrt(DM)
    strength = math.sqrt(300.0 * math.sqrt(HD)) / (0.714 * math.sqrt(DM))
    planted = strength * (token_signs / math.sqrt(DM))[:, None] * head_dir[None, :]
    return (drawn + planted).astype(jnp.bfloat16)


def draw_features(key, part):
    shuffled = jax.random.permutation(jax.random.fold_in(key, 21), TILES)
    tile_scale = 0.5 * 4.0 ** (shuffled.astype(jnp.float32) / (TILES - 1))
    shape = (TILES, CELLS, CELLS, CH)
    base = jnp.clip(jax.random.normal(jax.random.fold_in(key, 22), shape, jnp.float32), -4.0, 4.0)
    return (base * tile_scale[:, None, None, None]).astype(jnp.bfloat16)


def draw_patch_weight(key, part):
    token_signs, head_dir = shared_pattern(key)
    fan = PATCH * PATCH * CH
    drawn = bounded_normal(jax.random.fold_in(key, 31), (fan, DM)) / math.sqrt(fan)
    return (drawn + token_signs[None, :] / fan).astype(jnp.bfloat16)


def draw_query_weight(key, part):
    return drawn_projection(key, 41)


def draw_key_weight(key, part):
    return drawn_projection(key, 51)


def levels(own_key, extent, shards, least, largest):
    loudness, own = 1.0, jax.random.fold_in(own_key, 6)
    for position, blocks in shards:
        steps = jnp.exp(jax.random.uniform(jax.random.fold_in(own, position), (blocks,), jnp.float32, least / len(shards), largest / len(shards)))
        loudness = loudness * jnp.repeat(steps, extent[position] // blocks).reshape([-1 if axis == position else 1 for axis in range(len(extent))])
    return loudness


def gaussian(own_key, dims, spread, bound, cuts=(), held_as=jnp.bfloat16):
    entries = jax.random.normal(own_key, dims, jnp.float32) * spread
    if len(cuts) > 0:
        entries = levels(own_key, dims, cuts, -0.22, 0.18) * entries
    return jnp.clip(entries, min=-bound, max=bound).astype(held_as)


def setup_inputs(seed: int = 0, part: int = 0) -> dict:
    splits = jax.random.split(jax.random.key(seed), 10)
    part_keys = jax.random.split(jax.random.fold_in(splits[9], part), 10)
    features = draw_features(jax.random.fold_in(jax.random.fold_in(splits[9], part), 71), part)
    neighbours = draw_neighbours(jax.random.fold_in(jax.random.fold_in(splits[9], part), 71), part)
    conv_weight = gaussian(splits[2], (3, 3, CH, CH), (9 * CH) ** -0.5, 0.125)
    patch_weight = draw_patch_weight(jax.random.fold_in(splits[9], 71), part)
    query_weight = draw_query_weight(jax.random.fold_in(splits[9], 71), part)
    key_weight = draw_key_weight(jax.random.fold_in(splits[9], 71), part)
    value_weight = gaussian(splits[6], (DM, DM), DM ** -0.5, 0.21875)
    output_weight = gaussian(splits[7], (DM, DM), DM ** -0.5, 0.21875)
    cotangent = gaussian(part_keys[8], (TOKENS, DM), 1.0, 6.0, ((0, 16),))
    return {"features": features, "neighbours": neighbours, "conv_weight": conv_weight, "patch_weight": patch_weight, "query_weight": query_weight, "key_weight": key_weight, "value_weight": value_weight, "output_weight": output_weight, "cotangent": cotangent}


def tile_faces(maps):
    return jnp.stack([maps[:, 0], maps[:, -1], maps[:, :, 0], maps[:, :, -1]], axis=1)


def pad_tiles(maps, all_faces, links):
    upper = all_faces[links[:, 1], 1]
    lower = all_faces[links[:, 6], 0]
    left_col = all_faces[links[:, 3], 3]
    right_col = all_faces[links[:, 4], 2]
    corner_ul = all_faces[links[:, 0], 1, -1]
    corner_ur = all_faces[links[:, 2], 1, 0]
    corner_dl = all_faces[links[:, 5], 0, -1]
    corner_dr = all_faces[links[:, 7], 0, 0]
    top_row = jnp.concatenate([corner_ul[:, None], upper, corner_ur[:, None]], axis=1)
    bottom_row = jnp.concatenate([corner_dl[:, None], lower, corner_dr[:, None]], axis=1)
    middle = jnp.concatenate([left_col[:, :, None], maps, right_col[:, :, None]], axis=2)
    return jnp.concatenate([top_row[:, None], middle, bottom_row[:, None]], axis=1)


def conv_tiles(padded, kernel):
    count = padded.shape[0]
    side = padded.shape[1] - 2
    chans = padded.shape[3]
    total = jnp.zeros((count * side * side, kernel.shape[3]), jnp.float32)
    for row_off in range(3):
        for col_off in range(3):
            window = padded[:, row_off:row_off + side, col_off:col_off + side, :].reshape(-1, chans)
            total = total + jnp.dot(window, kernel[row_off, col_off], preferred_element_type=jnp.float32)
    return jax.nn.gelu(total).astype(jnp.bfloat16).reshape(count, side, side, -1)


def patchify(hidden, patch):
    count, side, _, chans = hidden.shape
    blocks = side // patch
    grid = hidden.reshape(count, blocks, patch, blocks, patch, chans).transpose(0, 1, 3, 2, 4, 5)
    return grid.reshape(count * blocks * blocks, patch * patch * chans)


def reference(features, neighbours, conv_weight, patch_weight, query_weight, key_weight, value_weight, output_weight, cotangent):
    all_faces = jnp.concatenate([tile_faces(features), jnp.zeros((1, 4, CELLS, CH), jnp.bfloat16)], axis=0)
    padded = pad_tiles(features, all_faces, neighbours)
    hidden = conv_tiles(padded, conv_weight)
    tokens = jnp.dot(patchify(hidden, PATCH), patch_weight, preferred_element_type=jnp.float32).astype(jnp.bfloat16)
    query = jnp.dot(tokens, query_weight, preferred_element_type=jnp.float32).astype(jnp.bfloat16)
    keys = jnp.dot(tokens, key_weight, preferred_element_type=jnp.float32).astype(jnp.bfloat16)
    values = jnp.dot(tokens, value_weight, preferred_element_type=jnp.float32).astype(jnp.bfloat16)
    keys_f = keys.astype(jnp.float32).reshape(TOKENS, HEADS, HD)
    values_f = values.astype(jnp.float32).reshape(TOKENS, HEADS, HD)
    scale = HD ** -0.5

    def attend_block(query_block):
        scores = jnp.einsum("qhd,khd->hqk", query_block.astype(jnp.float32), keys_f) * scale
        weights = jax.nn.softmax(scores, axis=-1).astype(jnp.bfloat16).astype(jnp.float32)
        return jnp.einsum("hqk,khd->qhd", weights, values_f)

    blocks = query.reshape(N_TILE, TOK_DEV, HEADS, HD)
    attended = lax.map(attend_block, blocks).reshape(TOKENS, DM).astype(jnp.bfloat16)
    mixed = (tokens.astype(jnp.float32) + jnp.dot(attended, output_weight, preferred_element_type=jnp.float32)).astype(jnp.bfloat16)
    output_grad = jnp.dot(attended.T, cotangent, preferred_element_type=jnp.float32)
    return mixed, output_grad
```

```python
import functools
import math

import jax
import jax.numpy as jnp
from jax import lax
from jax.experimental import pallas as pl
from jax.experimental.pallas import tpu as pltpu
from jax.sharding import PartitionSpec as P

PATCH = 4
HEADS = 12
HD = 64
GROUP = 4
GH = HEADS // GROUP
GW = GH * HD
MESH = pl.DeviceIdType.MESH
F32 = jnp.float32
BF16 = jnp.bfloat16


def remote(src, dst, send, recv, device):
    return pltpu.make_async_remote_copy(
        src_ref=src,
        dst_ref=dst,
        send_sem=send,
        recv_sem=recv,
        device_id={"tile": device},
        device_id_type=MESH,
    )


def place():
    me = lax.axis_index("tile")
    return me, me // GROUP, me % GROUP


def plane_partners(p):
    px = p + 1 - 2 * (p % 2)
    py = p + 2 - 4 * (p // 2)
    return px, py, GROUP - 1 - p


def when(cond, body):
    if isinstance(cond, bool):
        if cond:
            body()
    else:
        pl.when(cond)(body)


def stage_blocks(c, cols, s):
    if s == 0:
        return [(c, True, True, True)]
    return [(c - s, c - s >= 0, True, False), (c + s, c + s < cols, False, True)]


def gather_all(buf, cols, ss, rs):
    me, c, p = place()
    px, py, pd = plane_partners(p)

    def full(k, q):
        return buf.at[pl.ds(2 * (k * GROUP + q), 2)]

    def half(k, q, h):
        return buf.at[2 * (k * GROUP + q) + h]

    def z_copy(k, d):
        to = c + 1 - 2 * d
        return remote(full(k, p), full(k, p), ss.at[d, k], rs.at[0, k], to * GROUP + p)

    def x_copy(k, q):
        return remote(full(k, q), full(k, q), ss.at[2, k], rs.at[1, k], c * GROUP + px)

    def y_copy(k, q):
        return remote(full(k, q), full(k, q), ss.at[3, k], rs.at[2, k], c * GROUP + py)

    def y_pass(k, q):
        return remote(half(k, q, 0), half(k, q, 0), ss.at[4, k], rs.at[3, k], c * GROUP + py)

    def x_pass(k, q):
        return remote(half(k, q, 1), half(k, q, 1), ss.at[5, k], rs.at[4, k], c * GROUP + px)

    def pass_on(s):
        for k, ok, _, _ in stage_blocks(c, cols, s):
            def body(k=k):
                x_copy(k, px).wait_recv()
                y_pass(k, px).start()
                y_copy(k, py).wait_recv()
                x_pass(k, py).start()
            when(ok, body)

    for s in range(cols):
        for k, ok, up, down in stage_blocks(c, cols, s):
            def body(k=k, up=up, down=down):
                if s > 0:
                    z_copy(k, 0).wait_recv()
                if s < cols - 1:
                    if up:
                        when(c + 1 < cols, lambda: z_copy(k, 0).start())
                    if down:
                        when(c >= 1, lambda: z_copy(k, 1).start())
                x_copy(k, p).start()
                y_copy(k, p).start()
            when(ok, body)
        if s > 0:
            pass_on(s - 1)
    pass_on(cols - 1)
    for k in range(cols):
        y_pass(k, pd).wait_recv()
        x_pass(k, pd).wait_recv()
    for s in range(cols):
        for k, ok, up, down in stage_blocks(c, cols, s):
            def body(k=k, up=up, down=down):
                if s < cols - 1:
                    if up:
                        when(c + 1 < cols, lambda: z_copy(k, 0).wait_send())
                    if down:
                        when(c >= 1, lambda: z_copy(k, 1).wait_send())
                x_copy(k, p).wait_send()
                y_copy(k, p).wait_send()
                y_pass(k, px).wait_send()
                x_pass(k, py).wait_send()
            when(ok, body)


def embed_kernel(
    cols, x_ref, own_ref, nb_ref, cw_ref, pw_hbm, wq_hbm, wk_hbm, wv_hbm,
    tok_ref, kv_ref, q_ref,
    faces, ep, pw, ww, ss, rs, local_sem,
):
    n = cols * GROUP
    me, c, p = place()
    px, py, pd = plane_partners(p)
    loads = [
        pltpu.make_async_copy(x_ref, ep.at[pl.ds(1, 4), pl.ds(1, 4)], local_sem.at[0]),
        pltpu.make_async_copy(pw_hbm, pw, local_sem.at[1]),
        pltpu.make_async_copy(wq_hbm, ww.at[0], local_sem.at[2]),
        pltpu.make_async_copy(wk_hbm, ww.at[1], local_sem.at[3]),
        pltpu.make_async_copy(wv_hbm, ww.at[2], local_sem.at[4]),
    ]
    for load in loads:
        load.start()
    barrier = pltpu.get_barrier_semaphore()
    pl.semaphore_signal(barrier, inc=1, device_id={"tile": c * GROUP + px}, device_id_type=MESH)
    pl.semaphore_signal(barrier, inc=1, device_id={"tile": c * GROUP + py}, device_id_type=MESH)

    @pl.when(c + 1 < cols)
    def _():
        pl.semaphore_signal(barrier, inc=1, device_id={"tile": me + GROUP}, device_id_type=MESH)

    @pl.when(c >= 1)
    def _():
        pl.semaphore_signal(barrier, inc=1, device_id={"tile": me - GROUP}, device_id_type=MESH)

    faces[pl.ds(2 * me, 2)] = own_ref[...]
    faces[2 * n] = jnp.zeros_like(faces[2 * n])
    inner = (c >= 1) & (c + 1 < cols)

    @pl.when(inner)
    def _():
        pl.semaphore_wait(barrier, 4)

    @pl.when(jnp.logical_not(inner))
    def _():
        pl.semaphore_wait(barrier, 3)

    gather_all(faces, cols, ss, rs)

    loads[0].wait()
    ch = ep.shape[3]
    first = lax.broadcasted_iota(jnp.int32, (64, ch), 0) % 8

    def spread(col):
        return jnp.broadcast_to(col[:, None, :], (8, 8, ch)).reshape(64, ch)

    for t in range(2):
        rows = pl.ds(t * 64, 64)

        def face(link, which):
            return faces[nb_ref[t, link], which].astype(F32)

        upper = face(1, 1)
        lower = face(6, 0)
        left = face(3, 3)
        right = face(4, 2)
        corner_ul = face(0, 1)[31:32]
        corner_ur = face(2, 1)[0:1]
        corner_dl = face(5, 0)[31:32]
        corner_dr = face(7, 0)[0:1]
        for b in range(4):
            part = slice(b * 8, b * 8 + 8)
            above = jnp.concatenate([upper[part], ep[4, b + 1, rows].astype(F32)[0:56]], axis=0)
            below = jnp.concatenate([ep[1, b + 1, rows].astype(F32)[8:64], lower[part]], axis=0)
            ep[0, b + 1, rows] = above.astype(BF16)
            ep[5, b + 1, rows] = below.astype(BF16)
        lefts = [jnp.concatenate([corner_ul, left[24:31]], axis=0)]
        rights = [jnp.concatenate([corner_ur, right[24:31]], axis=0)]
        for a in range(4):
            lefts.append(left[a * 8:a * 8 + 8])
            rights.append(right[a * 8:a * 8 + 8])
        lefts.append(jnp.concatenate([left[1:8], corner_dl], axis=0))
        rights.append(jnp.concatenate([right[1:8], corner_dr], axis=0))
        for a in range(6):
            west = pltpu.roll(ep[a, 4, rows].astype(F32), 1, 0)
            east = pltpu.roll(ep[a, 1, rows].astype(F32), 63, 0)
            ep[a, 0, rows] = jnp.where(first == 0, spread(lefts[a]), west).astype(BF16)
            ep[a, 5, rows] = jnp.where(first == 7, spread(rights[a]), east).astype(BF16)

    loads[1].wait()
    tok = jnp.zeros(tok_ref.shape, F32)
    for i in range(4):
        acc = jnp.zeros((512, ch), F32)
        for dy in range(3):
            for dx in range(3):
                acc = acc + jnp.dot(
                    ep[i + dy, dx:dx + 4].reshape(512, ch), cw_ref[dy * 3 + dx],
                    preferred_element_type=F32,
                )
        hidden = jax.nn.gelu(acc).astype(BF16)
        wide = jnp.concatenate([hidden[j * 128:(j + 1) * 128] for j in range(4)], axis=1)
        tok = tok + jnp.dot(
            wide, pw[i * 4 * ch:(i + 1) * 4 * ch], preferred_element_type=F32
        )
    tokens = tok.astype(BF16)
    tok_ref[...] = tokens
    for load in loads[2:]:
        load.wait()
    query = jnp.dot(tokens, ww[0], preferred_element_type=F32)
    keys = jnp.dot(tokens, ww[1], preferred_element_type=F32)
    values = jnp.dot(tokens, ww[2], preferred_element_type=F32)
    for g in range(GROUP):
        part = slice(g * GW, (g + 1) * GW)
        q_ref[g] = query[:, part].astype(BF16)
        kv_ref[g] = jnp.concatenate([keys[:, part], values[:, part]], axis=1).astype(BF16)


def attend_kernel(
    cols, own_rows, tok_ref, kv_ref, q_ref, cot_ref, wo_ref,
    mixed_ref, grad_ref,
    kvg, qg, og, ogr, cotg, part_f, part_s, part_r, gr,
    kv_ss, kv_rs, q_ss, q_rs, c_ss, c_rs, o_ss, o_rs, z_ss, z_rs, p_ss, p_rs, ss, rs,
):
    n = cols * GROUP
    owners = GW // own_rows
    me, c, p = place()
    barrier = pltpu.get_barrier_semaphore()
    for d in range(1, GROUP):
        pl.semaphore_signal(
            barrier, inc=1, device_id={"tile": c * GROUP + (p + d) % GROUP}, device_id_type=MESH
        )
    for d in range(1, cols):
        pl.semaphore_signal(
            barrier, inc=1, device_id={"tile": (c + d) % cols * GROUP + p}, device_id_type=MESH
        )
    kvg[me] = kv_ref[p]
    qg[p] = q_ref[p]
    cotg[p] = cot_ref[...]
    pl.semaphore_wait(barrier, GROUP - 1 + cols - 1)

    def kv_plane(d):
        g = (p + d) % GROUP
        return remote(kv_ref.at[g], kvg.at[me], kv_ss.at[d], kv_rs.at[d], c * GROUP + g)

    def q_plane(d):
        g = (p + d) % GROUP
        return remote(q_ref.at[g], qg.at[p], q_ss.at[d], q_rs.at[d], c * GROUP + g)

    def c_plane(d):
        g = (p + d) % GROUP
        return remote(cotg.at[p], cotg.at[p], c_ss.at[d], c_rs.at[d], c * GROUP + g)

    def z_copy(k, d, way):
        b = k * GROUP + (p + GROUP - d) % GROUP
        to = c + 1 - 2 * way
        return remote(kvg.at[b], kvg.at[b], z_ss.at[way, k, d], z_rs.at[k, d], to * GROUP + p)

    for d in range(1, GROUP):
        kv_plane(d).start()
    for d in range(1, GROUP):
        q_plane(d).start()
    for s in range(cols):
        for d in range(GROUP):
            for k, ok, up, down in stage_blocks(c, cols, s):
                def body(k=k, up=up, down=down):
                    if s > 0:
                        z_copy(k, d, 0).wait_recv()
                    elif d > 0:
                        kv_plane(d).wait_recv()
                    if s < cols - 1:
                        if up:
                            when(c + 1 < cols, lambda: z_copy(k, d, 0).start())
                        if down:
                            when(c >= 1, lambda: z_copy(k, d, 1).start())
                when(ok, body)
        if s == 0:
            for d in range(1, GROUP):
                c_plane(d).start()
    for d in range(1, GROUP):
        q_plane(d).wait_recv()

    factor = HD ** (-0.5) * math.log2(math.e)

    def o_plane(d):
        g = (p + d) % GROUP
        return remote(og.at[g], ogr.at[p], o_ss.at[d], o_rs.at[d], c * GROUP + g)

    def attend(i, carry):
        g = (p + 1 + i) % GROUP
        for h in range(GH):
            lanes = slice(h * HD, (h + 1) * HD)
            key = kvg[:, :, lanes].reshape(n * 128, HD)
            value = kvg[:, :, GW + h * HD:GW + (h + 1) * HD].reshape(n * 128, HD)
            query = qg[g, :, lanes]
            scores = lax.dot_general(
                query, key, (((1,), (1,)), ((), ())), preferred_element_type=F32
            )
            top = jnp.max(scores, axis=1, keepdims=True)
            weights = jnp.exp2((scores - top) * factor)
            total = jnp.sum(weights, axis=1, keepdims=True)
            out = jnp.dot(weights.astype(BF16), value, preferred_element_type=F32)
            og[g, :, lanes] = (out / total).astype(BF16)

        return carry

    lax.fori_loop(0, GROUP, attend, 0)
    for d in range(1, GROUP):
        o_plane(d).start()
    for d in range(1, GROUP):
        c_plane(d).wait_recv()
    part = lax.dot_general(
        og[...].reshape(GROUP * 128, GW), cotg[...].reshape(GROUP * 128, -1),
        (((0,), (0,)), ((), ())), preferred_element_type=F32,
    )
    part_f[...] = part.reshape(part_f.shape)
    part_s[...] = part.reshape(part_f.shape).astype(BF16)

    def p_copy(d):
        j = (c + d) % cols
        return j, remote(
            part_s.at[j], part_r.at[d], p_ss.at[d], p_rs.at[d], j * GROUP + p
        )

    for d in range(1, cols):
        j, copy = p_copy(d)
        when(j < owners if owners < cols else True, copy.start)
    ogr[p] = og[p]
    for d in range(1, GROUP):
        o_plane(d).wait_recv()
    total = tok_ref[...].astype(F32)
    for g in range(GROUP):
        total = total + jnp.dot(
            ogr[g], wo_ref[g * GW:(g + 1) * GW], preferred_element_type=F32
        )
    mixed_ref[...] = total.astype(BF16)

    def reduce():
        acc = part_f[c]
        for d in range(1, cols):
            p_copy(d)[1].wait_recv()
            acc = acc + part_r[d].astype(F32)
        wide = acc.shape[1] // 2
        gr[2 * me] = acc[:, :wide].astype(BF16)
        gr[2 * me + 1] = acc[:, wide:].astype(BF16)

    def nothing():
        gr[2 * me] = jnp.zeros(gr.shape[1:], BF16)
        gr[2 * me + 1] = jnp.zeros(gr.shape[1:], BF16)

    if owners < cols:
        pl.when(c < owners)(reduce)
        pl.when(c >= owners)(nothing)
    else:
        reduce()
    gather_all(gr, cols, ss, rs)
    grad_ref[...] = gr[...]

    for d in range(1, GROUP):
        kv_plane(d).wait_send()
        q_plane(d).wait_send()
        c_plane(d).wait_send()
        o_plane(d).wait_send()
    for d in range(1, cols):
        j, copy = p_copy(d)
        when(j < owners if owners < cols else True, copy.wait_send)
    for s in range(cols - 1):
        for d in range(GROUP):
            for k, ok, up, down in stage_blocks(c, cols, s):
                def body(k=k, up=up, down=down):
                    if up:
                        when(c + 1 < cols, lambda: z_copy(k, d, 0).wait_send())
                    if down:
                        when(c >= 1, lambda: z_copy(k, d, 1).wait_send())
                when(ok, body)


def local(
    n, features, neighbours, conv_weight, patch_weight, query_weight, key_weight,
    value_weight, output_weight, cotangent,
):
    cols = n // GROUP
    tiles, side, _, ch = features.shape
    blocks = side // PATCH
    dm = query_weight.shape[0]
    rows = tiles * blocks * blocks
    vmem = pl.BlockSpec(memory_space=pltpu.VMEM)
    anyw = pl.BlockSpec(memory_space=pl.ANY)
    dma = pltpu.SemaphoreType.DMA

    x = features.reshape(tiles, blocks, PATCH, blocks, PATCH, ch).transpose(2, 4, 0, 1, 3, 5)
    own = jnp.stack(
        [
            x[0, :, :, 0].transpose(1, 0, 2, 3),
            x[-1, :, :, -1].transpose(1, 0, 2, 3),
            x[:, 0, :, :, 0].transpose(1, 0, 2, 3),
            x[:, -1, :, :, -1].transpose(1, 0, 2, 3),
        ],
        axis=1,
    ).reshape(tiles, 4, side, ch)
    x = x.reshape(PATCH, PATCH, rows, ch)

    tok, kv, q = pl.pallas_call(
        functools.partial(embed_kernel, cols),
        out_shape=(
            jax.ShapeDtypeStruct((rows, dm), BF16),
            jax.ShapeDtypeStruct((GROUP, rows, 2 * GW), BF16),
            jax.ShapeDtypeStruct((GROUP, rows, GW), BF16),
        ),
        in_specs=[anyw, vmem, pl.BlockSpec(memory_space=pltpu.SMEM), vmem, anyw, anyw, anyw, anyw],
        out_specs=(vmem, vmem, vmem),
        scratch_shapes=[
            pltpu.VMEM((2 * n + 1, 4, side, ch), BF16),
            pltpu.VMEM((6, 6, rows, ch), BF16),
            pltpu.VMEM(patch_weight.shape, BF16),
            pltpu.VMEM((3, dm, dm), BF16),
            dma((6, cols)),
            dma((5, cols)),
            dma((5,)),
        ],
        compiler_params=pltpu.CompilerParams(
            collective_id=0, has_side_effects=True, vmem_limit_bytes=52 * 2**20
        ),
        name="embed",
    )(
        x, own, neighbours, conv_weight.reshape(9, ch, ch), patch_weight,
        query_weight, key_weight, value_weight,
    )

    own_rows = max(16, GW // cols // 16 * 16)
    owners = GW // own_rows
    mixed, grad = pl.pallas_call(
        functools.partial(attend_kernel, cols, own_rows),
        out_shape=(
            jax.ShapeDtypeStruct((rows, dm), BF16),
            jax.ShapeDtypeStruct((2 * n, own_rows, dm // 2), BF16),
        ),
        in_specs=[vmem] * 5,
        out_specs=(vmem, vmem),
        scratch_shapes=[
            pltpu.VMEM((n, rows, 2 * GW), BF16),
            pltpu.VMEM((GROUP, rows, GW), BF16),
            pltpu.VMEM((GROUP, rows, GW), BF16),
            pltpu.VMEM((GROUP, rows, GW), BF16),
            pltpu.VMEM((GROUP, rows, dm), BF16),
            pltpu.VMEM((owners, own_rows, dm), F32),
            pltpu.VMEM((owners, own_rows, dm), BF16),
            pltpu.VMEM((cols, own_rows, dm), BF16),
            pltpu.VMEM((2 * n, own_rows, dm // 2), BF16),
            dma((GROUP,)), dma((GROUP,)),
            dma((GROUP,)), dma((GROUP,)),
            dma((GROUP,)), dma((GROUP,)),
            dma((GROUP,)), dma((GROUP,)),
            dma((2, cols, GROUP)), dma((cols, GROUP)),
            dma((cols,)), dma((cols,)),
            dma((6, cols)), dma((5, cols)),
        ],
        compiler_params=pltpu.CompilerParams(
            collective_id=1, has_side_effects=True, vmem_limit_bytes=52 * 2**20
        ),
        name="attend",
    )(tok, kv, q, cotangent, output_weight)

    output_grad = (
        grad.reshape(cols, GROUP, 2, own_rows, dm // 2)[:owners]
        .transpose(1, 0, 3, 2, 4)
        .reshape(dm, dm)
        .astype(F32)
    )
    return mixed, output_grad


def solution(mesh):
    part = P(("slide", "tile"))
    in_specs = (part, part) + (P(),) * 6 + (part,)
    out_specs = (part, P("slide"))
    return jax.shard_map(
        functools.partial(local, mesh.shape["tile"]),
        mesh=mesh, in_specs=in_specs, out_specs=out_specs, check_vma=False,
    )
```

```python
import functools
import math

import jax
import jax.numpy as jnp
from jax import lax
from jax.experimental import pallas as pl
from jax.experimental.pallas import tpu as pltpu
from jax.sharding import PartitionSpec as P

PATCH = 4
HEADS = 12
HD = 64
GROUP = 4
GH = HEADS // GROUP
GW = GH * HD
MESH = pl.DeviceIdType.MESH
F32 = jnp.float32
BF16 = jnp.bfloat16


def remote(src, dst, send, recv, device):
    return pltpu.make_async_remote_copy(
        src_ref=src,
        dst_ref=dst,
        send_sem=send,
        recv_sem=recv,
        device_id={"tile": device},
        device_id_type=MESH,
    )


def place():
    me = lax.axis_index("tile")
    return me, me // GROUP, me % GROUP


def plane_partners(p):
    px = p + 1 - 2 * (p % 2)
    py = p + 2 - 4 * (p // 2)
    return px, py, GROUP - 1 - p


def when(cond, body):
    if isinstance(cond, bool):
        if cond:
            body()
    else:
        pl.when(cond)(body)


def stage_blocks(c, cols, s):
    if s == 0:
        return [(c, True, True, True)]
    return [(c - s, c - s >= 0, True, False), (c + s, c + s < cols, False, True)]


def gather_steps(full, half, cols, ss, rs):
    me, c, p = place()
    px, py, pd = plane_partners(p)

    def z_copy(k, d):
        to = c + 1 - 2 * d
        return remote(full(k, p), full(k, p), ss(d, k), rs(0, k), to * GROUP + p)

    def x_copy(k, q):
        return remote(full(k, q), full(k, q), ss(2, k), rs(1, k), c * GROUP + px)

    def y_copy(k, q):
        return remote(full(k, q), full(k, q), ss(3, k), rs(2, k), c * GROUP + py)

    def y_pass(k, q):
        return remote(half(k, q, 0), half(k, q, 0), ss(4, k), rs(3, k), c * GROUP + py)

    def x_pass(k, q):
        return remote(half(k, q, 1), half(k, q, 1), ss(5, k), rs(4, k), c * GROUP + px)

    def pass_on(s):
        for k, ok, _, _ in stage_blocks(c, cols, s):
            def body(k=k):
                x_copy(k, px).wait_recv()
                y_pass(k, px).start()
                y_copy(k, py).wait_recv()
                x_pass(k, py).start()
            when(ok, body)

    for s in range(cols):
        for k, ok, up, down in stage_blocks(c, cols, s):
            def body(k=k, up=up, down=down):
                if s > 0:
                    z_copy(k, 0).wait_recv()
                if s < cols - 1:
                    if up:
                        when(c + 1 < cols, lambda: z_copy(k, 0).start())
                    if down:
                        when(c >= 1, lambda: z_copy(k, 1).start())
                x_copy(k, p).start()
                y_copy(k, p).start()
            when(ok, body)
        if s > 0:
            pass_on(s - 1)
        yield
    pass_on(cols - 1)
    yield
    for k in range(cols):
        y_pass(k, pd).wait_recv()
        x_pass(k, pd).wait_recv()
    for s in range(cols):
        for k, ok, up, down in stage_blocks(c, cols, s):
            def body(k=k, up=up, down=down):
                if s < cols - 1:
                    if up:
                        when(c + 1 < cols, lambda: z_copy(k, 0).wait_send())
                    if down:
                        when(c >= 1, lambda: z_copy(k, 1).wait_send())
                x_copy(k, p).wait_send()
                y_copy(k, p).wait_send()
                y_pass(k, px).wait_send()
                x_pass(k, py).wait_send()
            when(ok, body)


def advance(steps):
    return next(steps, "end") != "end"


def drain(*many):
    live = list(many)
    while live:
        live = [steps for steps in live if advance(steps)]


def embed_kernel(
    cols, x_ref, own_ref, nb_ref, cw_ref, pw_hbm, wq_hbm, wk_hbm, wv_hbm,
    tok_ref, kv_ref, q_ref,
    faces, ep, pw, ww, ss, rs, local_sem,
):
    n = cols * GROUP
    me, c, p = place()
    px, py, pd = plane_partners(p)
    loads = [
        pltpu.make_async_copy(x_ref, ep.at[pl.ds(1, 4), pl.ds(1, 4)], local_sem.at[0]),
        pltpu.make_async_copy(pw_hbm, pw, local_sem.at[1]),
        pltpu.make_async_copy(wq_hbm, ww.at[0], local_sem.at[2]),
        pltpu.make_async_copy(wk_hbm, ww.at[1], local_sem.at[3]),
        pltpu.make_async_copy(wv_hbm, ww.at[2], local_sem.at[4]),
    ]
    for load in loads:
        load.start()
    barrier = pltpu.get_barrier_semaphore()
    pl.semaphore_signal(barrier, inc=1, device_id={"tile": c * GROUP + px}, device_id_type=MESH)
    pl.semaphore_signal(barrier, inc=1, device_id={"tile": c * GROUP + py}, device_id_type=MESH)

    @pl.when(c + 1 < cols)
    def _():
        pl.semaphore_signal(barrier, inc=1, device_id={"tile": me + GROUP}, device_id_type=MESH)

    @pl.when(c >= 1)
    def _():
        pl.semaphore_signal(barrier, inc=1, device_id={"tile": me - GROUP}, device_id_type=MESH)

    faces[pl.ds(2 * me, 2)] = own_ref[...]
    faces[2 * n] = jnp.zeros_like(faces[2 * n])
    inner = (c >= 1) & (c + 1 < cols)

    @pl.when(inner)
    def _():
        pl.semaphore_wait(barrier, 4)

    @pl.when(jnp.logical_not(inner))
    def _():
        pl.semaphore_wait(barrier, 3)

    drain(gather_steps(
        lambda k, q: faces.at[pl.ds(2 * (k * GROUP + q), 2)],
        lambda k, q, h: faces.at[2 * (k * GROUP + q) + h],
        cols, lambda i, k: ss.at[i, k], lambda i, k: rs.at[i, k],
    ))

    loads[0].wait()
    ch = ep.shape[3]
    first = lax.broadcasted_iota(jnp.int32, (64, ch), 0) % 8

    def spread(col):
        return jnp.broadcast_to(col[:, None, :], (8, 8, ch)).reshape(64, ch)

    for t in range(2):
        rows = pl.ds(t * 64, 64)

        def face(link, which):
            return faces[nb_ref[t, link], which].astype(F32)

        upper = face(1, 1)
        lower = face(6, 0)
        left = face(3, 3)
        right = face(4, 2)
        corner_ul = face(0, 1)[31:32]
        corner_ur = face(2, 1)[0:1]
        corner_dl = face(5, 0)[31:32]
        corner_dr = face(7, 0)[0:1]
        for b in range(4):
            part = slice(b * 8, b * 8 + 8)
            above = jnp.concatenate([upper[part], ep[4, b + 1, rows].astype(F32)[0:56]], axis=0)
            below = jnp.concatenate([ep[1, b + 1, rows].astype(F32)[8:64], lower[part]], axis=0)
            ep[0, b + 1, rows] = above.astype(BF16)
            ep[5, b + 1, rows] = below.astype(BF16)
        lefts = [jnp.concatenate([corner_ul, left[24:31]], axis=0)]
        rights = [jnp.concatenate([corner_ur, right[24:31]], axis=0)]
        for a in range(4):
            lefts.append(left[a * 8:a * 8 + 8])
            rights.append(right[a * 8:a * 8 + 8])
        lefts.append(jnp.concatenate([left[1:8], corner_dl], axis=0))
        rights.append(jnp.concatenate([right[1:8], corner_dr], axis=0))
        for a in range(6):
            west = pltpu.roll(ep[a, 4, rows].astype(F32), 1, 0)
            east = pltpu.roll(ep[a, 1, rows].astype(F32), 63, 0)
            ep[a, 0, rows] = jnp.where(first == 0, spread(lefts[a]), west).astype(BF16)
            ep[a, 5, rows] = jnp.where(first == 7, spread(rights[a]), east).astype(BF16)

    loads[1].wait()
    tok = jnp.zeros(tok_ref.shape, F32)
    for i in range(4):
        acc = jnp.zeros((512, ch), F32)
        for dy in range(3):
            for dx in range(3):
                acc = acc + jnp.dot(
                    ep[i + dy, dx:dx + 4].reshape(512, ch), cw_ref[dy * 3 + dx],
                    preferred_element_type=F32,
                )
        hidden = jax.nn.gelu(acc).astype(BF16)
        wide = jnp.concatenate([hidden[j * 128:(j + 1) * 128] for j in range(4)], axis=1)
        tok = tok + jnp.dot(
            wide, pw[i * 4 * ch:(i + 1) * 4 * ch], preferred_element_type=F32
        )
    tokens = tok.astype(BF16)
    tok_ref[...] = tokens
    for load in loads[2:]:
        load.wait()
    query = jnp.dot(tokens, ww[0], preferred_element_type=F32)
    keys = jnp.dot(tokens, ww[1], preferred_element_type=F32)
    values = jnp.dot(tokens, ww[2], preferred_element_type=F32)
    for g in range(GROUP):
        part = slice(g * GW, (g + 1) * GW)
        q_ref[g] = query[:, part].astype(BF16)
        for h in range(GH):
            part = slice(g * GW + h * HD, g * GW + h * HD + HD)
            kv_ref[g, h] = jnp.concatenate([keys[:, part], values[:, part]], axis=1).astype(BF16)


def attend_kernel(
    cols, own_rows, tok_ref, kv_ref, q_ref, cot_ref, wo_ref,
    mixed_ref, grad_ref,
    kvg, qg, og, ogr, cotg, part_f, part_s, part_r, gr,
    kv_ss, kv_rs, q_ss, q_rs, c_ss, c_rs, o_ss, o_rs, z_ss, z_rs, p_ss, p_rs, ss, rs,
):
    n = cols * GROUP
    owners = HD // own_rows
    me, c, p = place()
    barrier = pltpu.get_barrier_semaphore()
    for d in range(1, GROUP):
        pl.semaphore_signal(
            barrier, inc=1, device_id={"tile": c * GROUP + (p + d) % GROUP}, device_id_type=MESH
        )
    for d in range(1, cols):
        pl.semaphore_signal(
            barrier, inc=1, device_id={"tile": (c + d) % cols * GROUP + p}, device_id_type=MESH
        )
    for h in range(GH):
        kvg[h, me] = kv_ref[p, h]
    qg[p] = q_ref[p]
    cotg[p] = cot_ref[...]
    pl.semaphore_wait(barrier, GROUP - 1 + cols - 1)

    def kv_plane(h, d):
        g = (p + d) % GROUP
        return remote(
            kv_ref.at[g, h], kvg.at[h, me], kv_ss.at[h, d], kv_rs.at[h, d], c * GROUP + g
        )

    def q_plane(d):
        g = (p + d) % GROUP
        return remote(q_ref.at[g], qg.at[p], q_ss.at[d], q_rs.at[d], c * GROUP + g)

    def c_plane(d):
        g = (p + d) % GROUP
        return remote(cotg.at[p], cotg.at[p], c_ss.at[d], c_rs.at[d], c * GROUP + g)

    def o_plane(d):
        g = (p + d) % GROUP
        return remote(og.at[g], ogr.at[p], o_ss.at[d], o_rs.at[d], c * GROUP + g)

    def z_copy(h, k, way):
        block = kvg.at[h, pl.ds(k * GROUP, GROUP)]
        to = c + 1 - 2 * way
        return remote(block, block, z_ss.at[h, way, k], z_rs.at[h, k], to * GROUP + p)

    def z_steps(h):
        for d in range(1, GROUP):
            kv_plane(h, d).wait_recv()
        for s in range(cols):
            for k, ok, up, down in stage_blocks(c, cols, s):
                def body(k=k, up=up, down=down):
                    if s > 0:
                        z_copy(h, k, 0).wait_recv()
                    if s < cols - 1:
                        if up:
                            when(c + 1 < cols, lambda: z_copy(h, k, 0).start())
                        if down:
                            when(c >= 1, lambda: z_copy(h, k, 1).start())
                when(ok, body)
            yield

    factor = HD ** (-0.5) * math.log2(math.e)

    def attend(h, first, last):
        lanes = slice(h * HD, (h + 1) * HD)

        def block(i, carry):
            g = (p + 1 + i) % GROUP
            key = kvg[h, :, :, 0:HD].reshape(n * 128, HD)
            value = kvg[h, :, :, HD:2 * HD].reshape(n * 128, HD)
            query = qg[g, :, lanes]
            scores = lax.dot_general(
                query, key, (((1,), (1,)), ((), ())), preferred_element_type=F32
            )
            top = jnp.max(scores, axis=1, keepdims=True)
            weights = jnp.exp2((scores - top) * factor)
            total = jnp.sum(weights, axis=1, keepdims=True)
            out = jnp.dot(weights.astype(BF16), value, preferred_element_type=F32)
            og[g, :, lanes] = (out / total).astype(BF16)
            return carry

        lax.fori_loop(first, last, block, 0)

    def p_copy(h, d):
        j = (c + d) % cols
        return j, remote(
            part_s.at[h, j], part_r.at[h, d], p_ss.at[h, d], p_rs.at[h, d], j * GROUP + p
        )

    def grad_steps(h):
        part = lax.dot_general(
            og[:, :, h * HD:(h + 1) * HD].reshape(GROUP * 128, HD),
            cotg[...].reshape(GROUP * 128, -1),
            (((0,), (0,)), ((), ())), preferred_element_type=F32,
        ).reshape(owners, own_rows, -1)
        part_f[h] = part
        part_s[h] = part.astype(BF16)
        for d in range(1, cols):
            j, copy = p_copy(h, d)
            when(j < owners if owners < cols else True, copy.start)
        yield

        def reduce():
            acc = part_f[h, c]
            for d in range(1, cols):
                p_copy(h, d)[1].wait_recv()
                acc = acc + part_r[h, d].astype(F32)
            gr[h, me] = acc.astype(BF16)

        def nothing():
            gr[h, me] = jnp.zeros(gr.shape[2:], BF16)

        if owners < cols:
            pl.when(c < owners)(reduce)
            pl.when(c >= owners)(nothing)
        else:
            reduce()
        wide = gr.shape[3] // 2
        yield from gather_steps(
            lambda k, q: gr.at[h, k * GROUP + q],
            lambda k, q, i: gr.at[h, k * GROUP + q, :, pl.ds(i * wide, wide)],
            cols, lambda i, k: ss.at[h, i, k], lambda i, k: rs.at[h, i, k],
        )
        for d in range(1, cols):
            j, copy = p_copy(h, d)
            when(j < owners if owners < cols else True, copy.wait_send)

    for h in range(GH):
        for d in range(1, GROUP):
            kv_plane(h, d).start()
        if h == 0:
            for d in range(1, GROUP):
                q_plane(d).start()
    for d in range(1, GROUP):
        c_plane(d).start()
    z = [z_steps(h) for h in range(GH)]
    grads = [grad_steps(h) for h in range(GH)]
    advance(z[0])
    advance(z[1])
    advance(z[0])
    advance(z[2])
    advance(z[0])
    advance(z[1])
    drain(z[0])
    for d in range(1, GROUP):
        q_plane(d).wait_recv()
    attend(0, 0, 2)
    advance(z[1])
    advance(z[2])
    attend(0, 2, 4)
    drain(z[1])
    advance(z[2])
    for d in range(1, GROUP):
        c_plane(d).wait_recv()
    advance(grads[0])
    attend(1, 0, 2)
    drain(z[2])
    advance(grads[0])
    attend(1, 2, 4)
    advance(grads[0])
    advance(grads[1])
    attend(2, 0, 2)
    advance(grads[0])
    advance(grads[1])
    attend(2, 2, 4)
    for d in range(1, GROUP):
        o_plane(d).start()
    advance(grads[2])
    advance(grads[0])
    advance(grads[1])
    ogr[p] = og[p]
    for d in range(1, GROUP):
        o_plane(d).wait_recv()
    total = tok_ref[...].astype(F32)
    for g in range(GROUP):
        total = total + jnp.dot(
            ogr[g], wo_ref[g * GW:(g + 1) * GW], preferred_element_type=F32
        )
    mixed_ref[...] = total.astype(BF16)
    drain(*grads)
    for q in range(GROUP):
        for h in range(GH):
            for k in range(owners):
                row = q * GW + h * HD + k * own_rows
                grad_ref[row:row + own_rows] = gr[h, k * GROUP + q]

    for d in range(1, GROUP):
        for h in range(GH):
            kv_plane(h, d).wait_send()
        q_plane(d).wait_send()
        c_plane(d).wait_send()
        o_plane(d).wait_send()
    for h in range(GH):
        for s in range(cols - 1):
            for k, ok, up, down in stage_blocks(c, cols, s):
                def body(k=k, up=up, down=down):
                    if up:
                        when(c + 1 < cols, lambda: z_copy(h, k, 0).wait_send())
                    if down:
                        when(c >= 1, lambda: z_copy(h, k, 1).wait_send())
                when(ok, body)


def local(
    n, features, neighbours, conv_weight, patch_weight, query_weight, key_weight,
    value_weight, output_weight, cotangent,
):
    cols = n // GROUP
    tiles, side, _, ch = features.shape
    blocks = side // PATCH
    dm = query_weight.shape[0]
    rows = tiles * blocks * blocks
    vmem = pl.BlockSpec(memory_space=pltpu.VMEM)
    anyw = pl.BlockSpec(memory_space=pl.ANY)
    dma = pltpu.SemaphoreType.DMA

    x = features.reshape(tiles, blocks, PATCH, blocks, PATCH, ch).transpose(2, 4, 0, 1, 3, 5)
    own = jnp.stack(
        [
            x[0, :, :, 0].transpose(1, 0, 2, 3),
            x[-1, :, :, -1].transpose(1, 0, 2, 3),
            x[:, 0, :, :, 0].transpose(1, 0, 2, 3),
            x[:, -1, :, :, -1].transpose(1, 0, 2, 3),
        ],
        axis=1,
    ).reshape(tiles, 4, side, ch)
    x = x.reshape(PATCH, PATCH, rows, ch)

    tok, kv, q = pl.pallas_call(
        functools.partial(embed_kernel, cols),
        out_shape=(
            jax.ShapeDtypeStruct((rows, dm), BF16),
            jax.ShapeDtypeStruct((GROUP, GH, rows, 2 * HD), BF16),
            jax.ShapeDtypeStruct((GROUP, rows, GW), BF16),
        ),
        in_specs=[anyw, vmem, pl.BlockSpec(memory_space=pltpu.SMEM), vmem, anyw, anyw, anyw, anyw],
        out_specs=(vmem, vmem, vmem),
        scratch_shapes=[
            pltpu.VMEM((2 * n + 1, 4, side, ch), BF16),
            pltpu.VMEM((6, 6, rows, ch), BF16),
            pltpu.VMEM(patch_weight.shape, BF16),
            pltpu.VMEM((3, dm, dm), BF16),
            dma((6, cols)),
            dma((5, cols)),
            dma((5,)),
        ],
        compiler_params=pltpu.CompilerParams(
            collective_id=0, has_side_effects=True, vmem_limit_bytes=52 * 2**20
        ),
        name="embed",
    )(
        x, own, neighbours, conv_weight.reshape(9, ch, ch), patch_weight,
        query_weight, key_weight, value_weight,
    )

    own_rows = max(16, HD // cols // 16 * 16)
    owners = HD // own_rows
    mixed, grad = pl.pallas_call(
        functools.partial(attend_kernel, cols, own_rows),
        out_shape=(
            jax.ShapeDtypeStruct((rows, dm), BF16),
            jax.ShapeDtypeStruct((dm, dm), BF16),
        ),
        in_specs=[vmem] * 5,
        out_specs=(vmem, vmem),
        scratch_shapes=[
            pltpu.VMEM((GH, n, rows, 2 * HD), BF16),
            pltpu.VMEM((GROUP, rows, GW), BF16),
            pltpu.VMEM((GROUP, rows, GW), BF16),
            pltpu.VMEM((GROUP, rows, GW), BF16),
            pltpu.VMEM((GROUP, rows, dm), BF16),
            pltpu.VMEM((GH, owners, own_rows, dm), F32),
            pltpu.VMEM((GH, owners, own_rows, dm), BF16),
            pltpu.VMEM((GH, cols, own_rows, dm), BF16),
            pltpu.VMEM((GH, n, own_rows, dm), BF16),
            dma((GH, GROUP)), dma((GH, GROUP)),
            dma((GROUP,)), dma((GROUP,)),
            dma((GROUP,)), dma((GROUP,)),
            dma((GROUP,)), dma((GROUP,)),
            dma((GH, 2, cols)), dma((GH, cols)),
            dma((GH, cols)), dma((GH, cols)),
            dma((GH, 6, cols)), dma((GH, 5, cols)),
        ],
        compiler_params=pltpu.CompilerParams(
            collective_id=1, has_side_effects=True, vmem_limit_bytes=52 * 2**20
        ),
        name="attend",
    )(tok, kv, q, cotangent, output_weight)
    return mixed, grad.astype(F32)


def solution(mesh):
    part = P(("slide", "tile"))
    in_specs = (part, part) + (P(),) * 6 + (part,)
    out_specs = (part, P("slide"))
    return jax.shard_map(
        functools.partial(local, mesh.shape["tile"]),
        mesh=mesh, in_specs=in_specs, out_specs=out_specs, check_vma=False,
    )
```

```python
import functools
import math

import jax
import jax.numpy as jnp
from jax import lax
from jax.experimental import pallas as pl
from jax.experimental.pallas import tpu as pltpu
from jax.sharding import PartitionSpec as P

PATCH = 4
HEADS = 12
HD = 64
GROUP = 4
GH = HEADS // GROUP
GW = GH * HD
MESH = pl.DeviceIdType.MESH
F32 = jnp.float32
BF16 = jnp.bfloat16


def remote(src, dst, send, recv, device):
    return pltpu.make_async_remote_copy(
        src_ref=src,
        dst_ref=dst,
        send_sem=send,
        recv_sem=recv,
        device_id={"tile": device},
        device_id_type=MESH,
    )


def place():
    me = lax.axis_index("tile")
    return me, me // GROUP, me % GROUP


def plane_partners(p):
    px = p + 1 - 2 * (p % 2)
    py = p + 2 - 4 * (p // 2)
    return px, py, GROUP - 1 - p


def when(cond, body):
    if isinstance(cond, bool):
        if cond:
            body()
    else:
        pl.when(cond)(body)


def stage_blocks(c, cols, s):
    if s == 0:
        return [(c, True, True, True)]
    return [(c - s, c - s >= 0, True, False), (c + s, c + s < cols, False, True)]


def gather_steps(full, half, cols, ss, rs):
    me, c, p = place()
    px, py, pd = plane_partners(p)

    def z_copy(k, d):
        to = c + 1 - 2 * d
        return remote(full(k, p), full(k, p), ss(d, k), rs(0, k), to * GROUP + p)

    def x_copy(k, q):
        return remote(full(k, q), full(k, q), ss(2, k), rs(1, k), c * GROUP + px)

    def y_copy(k, q):
        return remote(full(k, q), full(k, q), ss(3, k), rs(2, k), c * GROUP + py)

    def y_pass(k, q):
        return remote(half(k, q, 0), half(k, q, 0), ss(4, k), rs(3, k), c * GROUP + py)

    def x_pass(k, q):
        return remote(half(k, q, 1), half(k, q, 1), ss(5, k), rs(4, k), c * GROUP + px)

    def pass_on(s):
        for k, ok, _, _ in stage_blocks(c, cols, s):
            def body(k=k):
                x_copy(k, px).wait_recv()
                y_pass(k, px).start()
                y_copy(k, py).wait_recv()
                x_pass(k, py).start()
            when(ok, body)

    for s in range(cols):
        for k, ok, up, down in stage_blocks(c, cols, s):
            def body(k=k, up=up, down=down):
                if s > 0:
                    z_copy(k, 0).wait_recv()
                if s < cols - 1:
                    if up:
                        when(c + 1 < cols, lambda: z_copy(k, 0).start())
                    if down:
                        when(c >= 1, lambda: z_copy(k, 1).start())
                x_copy(k, p).start()
                y_copy(k, p).start()
            when(ok, body)
        if s > 0:
            pass_on(s - 1)
        yield
    pass_on(cols - 1)
    yield
    for k in range(cols):
        y_pass(k, pd).wait_recv()
        x_pass(k, pd).wait_recv()
    for s in range(cols):
        for k, ok, up, down in stage_blocks(c, cols, s):
            def body(k=k, up=up, down=down):
                if s < cols - 1:
                    if up:
                        when(c + 1 < cols, lambda: z_copy(k, 0).wait_send())
                    if down:
                        when(c >= 1, lambda: z_copy(k, 1).wait_send())
                x_copy(k, p).wait_send()
                y_copy(k, p).wait_send()
                y_pass(k, px).wait_send()
                x_pass(k, py).wait_send()
            when(ok, body)


def direct_steps(full, cols, zs, zr, ps, pr):
    me, c, p = place()

    def z_copy(d, k):
        to = (c + d) % cols
        return remote(full(k, p), full(k, p), zs(d), zr(d), to * GROUP + p)

    def plane(d, e, q):
        k = (c + cols - d) % cols
        return remote(full(k, q), full(k, q), ps(d, e), pr(d, e), c * GROUP + (p + e) % GROUP)

    for d in range(1, cols):
        z_copy(d, c).start()
    for e in range(1, GROUP):
        plane(0, e, p).start()
    yield
    for d in range(1, cols):
        z_copy(d, (c + cols - d) % cols).wait_recv()
        for e in range(1, GROUP):
            plane(d, e, p).start()
    yield
    for d in range(cols):
        for e in range(1, GROUP):
            plane(d, e, (p + GROUP - e) % GROUP).wait_recv()
    for d in range(cols):
        if d:
            z_copy(d, c).wait_send()
        for e in range(1, GROUP):
            plane(d, e, p).wait_send()


def advance(steps):
    return next(steps, "end") != "end"


def drain(*many):
    live = list(many)
    while live:
        live = [steps for steps in live if advance(steps)]


def embed_kernel(
    cols, x_ref, own_ref, nb_ref, cw_ref, pw_hbm, wq_hbm, wk_hbm, wv_hbm,
    tok_ref, kv_ref, q_ref,
    faces, ep, pw, ww, ss, rs, local_sem,
):
    n = cols * GROUP
    me, c, p = place()
    px, py, pd = plane_partners(p)
    loads = [
        pltpu.make_async_copy(x_ref, ep.at[pl.ds(1, 4), pl.ds(1, 4)], local_sem.at[0]),
        pltpu.make_async_copy(pw_hbm, pw, local_sem.at[1]),
        pltpu.make_async_copy(wq_hbm, ww.at[0], local_sem.at[2]),
        pltpu.make_async_copy(wk_hbm, ww.at[1], local_sem.at[3]),
        pltpu.make_async_copy(wv_hbm, ww.at[2], local_sem.at[4]),
    ]
    for load in loads:
        load.start()
    barrier = pltpu.get_barrier_semaphore()
    pl.semaphore_signal(barrier, inc=1, device_id={"tile": c * GROUP + px}, device_id_type=MESH)
    pl.semaphore_signal(barrier, inc=1, device_id={"tile": c * GROUP + py}, device_id_type=MESH)

    @pl.when(c + 1 < cols)
    def _():
        pl.semaphore_signal(barrier, inc=1, device_id={"tile": me + GROUP}, device_id_type=MESH)

    @pl.when(c >= 1)
    def _():
        pl.semaphore_signal(barrier, inc=1, device_id={"tile": me - GROUP}, device_id_type=MESH)

    faces[pl.ds(2 * me, 2)] = own_ref[...]
    faces[2 * n] = jnp.zeros_like(faces[2 * n])
    inner = (c >= 1) & (c + 1 < cols)

    @pl.when(inner)
    def _():
        pl.semaphore_wait(barrier, 4)

    @pl.when(jnp.logical_not(inner))
    def _():
        pl.semaphore_wait(barrier, 3)

    drain(gather_steps(
        lambda k, q: faces.at[pl.ds(2 * (k * GROUP + q), 2)],
        lambda k, q, h: faces.at[2 * (k * GROUP + q) + h],
        cols, lambda i, k: ss.at[i, k], lambda i, k: rs.at[i, k],
    ))

    loads[0].wait()
    ch = ep.shape[3]
    first = lax.broadcasted_iota(jnp.int32, (64, ch), 0) % 8

    def spread(col):
        return jnp.broadcast_to(col[:, None, :], (8, 8, ch)).reshape(64, ch)

    for t in range(2):
        rows = pl.ds(t * 64, 64)

        def face(link, which):
            return faces[nb_ref[t, link], which].astype(F32)

        upper = face(1, 1)
        lower = face(6, 0)
        left = face(3, 3)
        right = face(4, 2)
        corner_ul = face(0, 1)[31:32]
        corner_ur = face(2, 1)[0:1]
        corner_dl = face(5, 0)[31:32]
        corner_dr = face(7, 0)[0:1]
        for b in range(4):
            part = slice(b * 8, b * 8 + 8)
            above = jnp.concatenate([upper[part], ep[4, b + 1, rows].astype(F32)[0:56]], axis=0)
            below = jnp.concatenate([ep[1, b + 1, rows].astype(F32)[8:64], lower[part]], axis=0)
            ep[0, b + 1, rows] = above.astype(BF16)
            ep[5, b + 1, rows] = below.astype(BF16)
        lefts = [jnp.concatenate([corner_ul, left[24:31]], axis=0)]
        rights = [jnp.concatenate([corner_ur, right[24:31]], axis=0)]
        for a in range(4):
            lefts.append(left[a * 8:a * 8 + 8])
            rights.append(right[a * 8:a * 8 + 8])
        lefts.append(jnp.concatenate([left[1:8], corner_dl], axis=0))
        rights.append(jnp.concatenate([right[1:8], corner_dr], axis=0))
        for a in range(6):
            west = pltpu.roll(ep[a, 4, rows].astype(F32), 1, 0)
            east = pltpu.roll(ep[a, 1, rows].astype(F32), 63, 0)
            ep[a, 0, rows] = jnp.where(first == 0, spread(lefts[a]), west).astype(BF16)
            ep[a, 5, rows] = jnp.where(first == 7, spread(rights[a]), east).astype(BF16)

    loads[1].wait()
    tok = jnp.zeros(tok_ref.shape, F32)
    for i in range(4):
        acc = jnp.zeros((512, ch), F32)
        for dy in range(3):
            for dx in range(3):
                acc = acc + jnp.dot(
                    ep[i + dy, dx:dx + 4].reshape(512, ch), cw_ref[dy * 3 + dx],
                    preferred_element_type=F32,
                )
        hidden = jax.nn.gelu(acc).astype(BF16)
        wide = jnp.concatenate([hidden[j * 128:(j + 1) * 128] for j in range(4)], axis=1)
        tok = tok + jnp.dot(
            wide, pw[i * 4 * ch:(i + 1) * 4 * ch], preferred_element_type=F32
        )
    tokens = tok.astype(BF16)
    tok_ref[...] = tokens
    for load in loads[2:]:
        load.wait()
    query = jnp.dot(tokens, ww[0], preferred_element_type=F32)
    keys = jnp.dot(tokens, ww[1], preferred_element_type=F32)
    values = jnp.dot(tokens, ww[2], preferred_element_type=F32)
    for g in range(GROUP):
        part = slice(g * GW, (g + 1) * GW)
        q_ref[g] = query[:, part].astype(BF16)
        for h in range(GH):
            part = slice(g * GW + h * HD, g * GW + h * HD + HD)
            kv_ref[g, h] = jnp.concatenate([keys[:, part], values[:, part]], axis=1).astype(BF16)


def attend_kernel(
    cols, own_rows, tok_ref, kv_ref, q_ref, cot_ref, wo_ref,
    mixed_ref, grad_ref,
    kvg, qg, og, ogr, cotg, part_f, part_s, part_r, gr,
    kv_ss, kv_rs, q_ss, q_rs, c_ss, c_rs, o_ss, o_rs, z_ss, z_rs, p_ss, p_rs, zs, zr, ss, rs,
):
    n = cols * GROUP
    owners = HD // own_rows
    me, c, p = place()
    barrier = pltpu.get_barrier_semaphore()
    for d in range(1, GROUP):
        pl.semaphore_signal(
            barrier, inc=1, device_id={"tile": c * GROUP + (p + d) % GROUP}, device_id_type=MESH
        )
    for d in range(1, cols):
        pl.semaphore_signal(
            barrier, inc=1, device_id={"tile": (c + d) % cols * GROUP + p}, device_id_type=MESH
        )
    for h in range(GH):
        kvg[h, me] = kv_ref[p, h]
    qg[p] = q_ref[p]
    cotg[p] = cot_ref[...]
    pl.semaphore_wait(barrier, GROUP - 1 + cols - 1)

    def kv_plane(h, d):
        g = (p + d) % GROUP
        return remote(
            kv_ref.at[g, h], kvg.at[h, me], kv_ss.at[h, d], kv_rs.at[h, d], c * GROUP + g
        )

    def q_plane(d):
        g = (p + d) % GROUP
        return remote(q_ref.at[g], qg.at[p], q_ss.at[d], q_rs.at[d], c * GROUP + g)

    def c_plane(d):
        g = (p + d) % GROUP
        return remote(cotg.at[p], cotg.at[p], c_ss.at[d], c_rs.at[d], c * GROUP + g)

    def o_plane(d):
        g = (p + d) % GROUP
        return remote(og.at[g], ogr.at[p], o_ss.at[d], o_rs.at[d], c * GROUP + g)

    def z_copy(h, k, way):
        block = kvg.at[h, pl.ds(k * GROUP, GROUP)]
        to = c + 1 - 2 * way
        return remote(block, block, z_ss.at[h, way, k], z_rs.at[h, k], to * GROUP + p)

    def z_steps(h):
        for d in range(1, GROUP):
            kv_plane(h, d).wait_recv()
        for s in range(cols):
            for k, ok, up, down in stage_blocks(c, cols, s):
                def body(k=k, up=up, down=down):
                    if s > 0:
                        z_copy(h, k, 0).wait_recv()
                    if s < cols - 1:
                        if up:
                            when(c + 1 < cols, lambda: z_copy(h, k, 0).start())
                        if down:
                            when(c >= 1, lambda: z_copy(h, k, 1).start())
                when(ok, body)
            yield

    factor = HD ** (-0.5) * math.log2(math.e)

    def attend(h, first, last):
        lanes = slice(h * HD, (h + 1) * HD)
        count = (last - first) * 128
        both = kvg[h].reshape(n * 128, 2 * HD)
        query = qg[first:last, :, lanes].reshape(count, HD)
        query = jnp.concatenate([query, jnp.zeros_like(query)], axis=1)
        scores = lax.dot_general(
            query, both, (((1,), (1,)), ((), ())), preferred_element_type=F32
        )
        top = jnp.max(scores, axis=1, keepdims=True)
        weights = jnp.exp2((scores - top) * factor)
        total = jnp.sum(weights, axis=1, keepdims=True)
        out = jnp.dot(weights.astype(BF16), both, preferred_element_type=F32)
        out = (out / total)[:, HD:].astype(BF16)
        og[first:last, :, lanes] = out.reshape(last - first, 128, HD)

    def p_copy(h, d):
        j = (c + d) % cols
        return j, remote(
            part_s.at[h, j], part_r.at[h, d], p_ss.at[h, d], p_rs.at[h, d], j * GROUP + p
        )

    def grad_steps(h):
        part = lax.dot_general(
            og[:, :, h * HD:(h + 1) * HD].reshape(GROUP * 128, HD),
            cotg[...].reshape(GROUP * 128, -1),
            (((0,), (0,)), ((), ())), preferred_element_type=F32,
        ).reshape(owners, own_rows, -1)
        part_f[h] = part
        part_s[h] = part.astype(BF16)
        for d in range(1, cols):
            j, copy = p_copy(h, d)
            when(j < owners if owners < cols else True, copy.start)
        yield

        def reduce():
            acc = part_f[h, c]
            for d in range(1, cols):
                p_copy(h, d)[1].wait_recv()
                acc = acc + part_r[h, d].astype(F32)
            gr[h, me] = acc.astype(BF16)

        def nothing():
            gr[h, me] = jnp.zeros(gr.shape[2:], BF16)

        if owners < cols:
            pl.when(c < owners)(reduce)
            pl.when(c >= owners)(nothing)
        else:
            reduce()
        yield from direct_steps(
            lambda k, q: gr.at[h, k * GROUP + q], cols,
            lambda d: zs.at[h, d], lambda d: zr.at[h, d],
            lambda d, e: ss.at[h, d, e], lambda d, e: rs.at[h, d, e],
        )
        for d in range(1, cols):
            j, copy = p_copy(h, d)
            when(j < owners if owners < cols else True, copy.wait_send)

    for h in range(GH):
        for d in range(1, GROUP):
            kv_plane(h, d).start()
        if h == 0:
            for d in range(1, GROUP):
                q_plane(d).start()
    for d in range(1, GROUP):
        c_plane(d).start()
    z = [z_steps(h) for h in range(GH)]
    grads = [grad_steps(h) for h in range(GH)]
    advance(z[0])
    advance(z[1])
    advance(z[0])
    advance(z[2])
    advance(z[0])
    advance(z[1])
    drain(z[0])
    for d in range(1, GROUP):
        q_plane(d).wait_recv()
    attend(0, 0, 2)
    advance(z[1])
    advance(z[2])
    attend(0, 2, 4)
    drain(z[1])
    advance(z[2])
    for d in range(1, GROUP):
        c_plane(d).wait_recv()
    advance(grads[0])
    attend(1, 0, 2)
    drain(z[2])
    advance(grads[0])
    attend(1, 2, 4)
    advance(grads[0])
    advance(grads[1])
    attend(2, 0, 2)
    advance(grads[1])
    attend(2, 2, 4)
    for d in range(1, GROUP):
        o_plane(d).start()
    advance(grads[2])
    advance(grads[1])
    ogr[p] = og[p]
    for d in range(1, GROUP):
        o_plane(d).wait_recv()
    total = tok_ref[...].astype(F32)
    for g in range(GROUP):
        total = total + jnp.dot(
            ogr[g], wo_ref[g * GW:(g + 1) * GW], preferred_element_type=F32
        )
    mixed_ref[...] = total.astype(BF16)
    advance(grads[2])
    drain(grads[0], grads[1], grads[2])
    for q in range(GROUP):
        for h in range(GH):
            for k in range(owners):
                row = q * GW + h * HD + k * own_rows
                grad_ref[row:row + own_rows] = gr[h, k * GROUP + q].astype(F32)

    for d in range(1, GROUP):
        for h in range(GH):
            kv_plane(h, d).wait_send()
        q_plane(d).wait_send()
        c_plane(d).wait_send()
        o_plane(d).wait_send()
    for h in range(GH):
        for s in range(cols - 1):
            for k, ok, up, down in stage_blocks(c, cols, s):
                def body(k=k, up=up, down=down):
                    if up:
                        when(c + 1 < cols, lambda: z_copy(h, k, 0).wait_send())
                    if down:
                        when(c >= 1, lambda: z_copy(h, k, 1).wait_send())
                when(ok, body)


def local(
    n, features, neighbours, conv_weight, patch_weight, query_weight, key_weight,
    value_weight, output_weight, cotangent,
):
    cols = n // GROUP
    tiles, side, _, ch = features.shape
    blocks = side // PATCH
    dm = query_weight.shape[0]
    rows = tiles * blocks * blocks
    vmem = pl.BlockSpec(memory_space=pltpu.VMEM)
    anyw = pl.BlockSpec(memory_space=pl.ANY)
    dma = pltpu.SemaphoreType.DMA

    x = features.reshape(tiles, blocks, PATCH, blocks, PATCH, ch).transpose(2, 4, 0, 1, 3, 5)
    own = jnp.stack(
        [
            x[0, :, :, 0].transpose(1, 0, 2, 3),
            x[-1, :, :, -1].transpose(1, 0, 2, 3),
            x[:, 0, :, :, 0].transpose(1, 0, 2, 3),
            x[:, -1, :, :, -1].transpose(1, 0, 2, 3),
        ],
        axis=1,
    ).reshape(tiles, 4, side, ch)
    x = x.reshape(PATCH, PATCH, rows, ch)

    tok, kv, q = pl.pallas_call(
        functools.partial(embed_kernel, cols),
        out_shape=(
            jax.ShapeDtypeStruct((rows, dm), BF16),
            jax.ShapeDtypeStruct((GROUP, GH, rows, 2 * HD), BF16),
            jax.ShapeDtypeStruct((GROUP, rows, GW), BF16),
        ),
        in_specs=[anyw, vmem, pl.BlockSpec(memory_space=pltpu.SMEM), vmem, anyw, anyw, anyw, anyw],
        out_specs=(vmem, vmem, vmem),
        scratch_shapes=[
            pltpu.VMEM((2 * n + 1, 4, side, ch), BF16),
            pltpu.VMEM((6, 6, rows, ch), BF16),
            pltpu.VMEM(patch_weight.shape, BF16),
            pltpu.VMEM((3, dm, dm), BF16),
            dma((6, cols)),
            dma((5, cols)),
            dma((5,)),
        ],
        compiler_params=pltpu.CompilerParams(
            collective_id=0, has_side_effects=True, vmem_limit_bytes=52 * 2**20
        ),
        name="embed",
    )(
        x, own, neighbours, conv_weight.reshape(9, ch, ch), patch_weight,
        query_weight, key_weight, value_weight,
    )

    own_rows = max(16, HD // cols // 16 * 16)
    owners = HD // own_rows
    mixed, grad = pl.pallas_call(
        functools.partial(attend_kernel, cols, own_rows),
        out_shape=(
            jax.ShapeDtypeStruct((rows, dm), BF16),
            jax.ShapeDtypeStruct((dm, dm), F32),
        ),
        in_specs=[vmem] * 5,
        out_specs=(vmem, vmem),
        scratch_shapes=[
            pltpu.VMEM((GH, n, rows, 2 * HD), BF16),
            pltpu.VMEM((GROUP, rows, GW), BF16),
            pltpu.VMEM((GROUP, rows, GW), BF16),
            pltpu.VMEM((GROUP, rows, GW), BF16),
            pltpu.VMEM((GROUP, rows, dm), BF16),
            pltpu.VMEM((GH, owners, own_rows, dm), F32),
            pltpu.VMEM((GH, owners, own_rows, dm), BF16),
            pltpu.VMEM((GH, cols, own_rows, dm), BF16),
            pltpu.VMEM((GH, n, own_rows, dm), BF16),
            dma((GH, GROUP)), dma((GH, GROUP)),
            dma((GROUP,)), dma((GROUP,)),
            dma((GROUP,)), dma((GROUP,)),
            dma((GROUP,)), dma((GROUP,)),
            dma((GH, 2, cols)), dma((GH, cols)),
            dma((GH, cols)), dma((GH, cols)),
            dma((GH, cols)), dma((GH, cols)),
            dma((GH, cols, GROUP)), dma((GH, cols, GROUP)),
        ],
        compiler_params=pltpu.CompilerParams(
            collective_id=1, has_side_effects=True, vmem_limit_bytes=52 * 2**20
        ),
        name="attend",
    )(tok, kv, q, cotangent, output_weight)
    return mixed, grad


def solution(mesh):
    part = P(("slide", "tile"))
    in_specs = (part, part) + (P(),) * 6 + (part,)
    out_specs = (part, P("slide"))
    return jax.shard_map(
        functools.partial(local, mesh.shape["tile"]),
        mesh=mesh, in_specs=in_specs, out_specs=out_specs, check_vma=False,
    )
```

```python
import functools
import math

import jax
import jax.numpy as jnp
from jax import lax
from jax.experimental import pallas as pl
from jax.experimental.pallas import tpu as pltpu
from jax.sharding import PartitionSpec as P

PATCH = 4
HEADS = 12
HD = 64
GROUP = 4
GH = HEADS // GROUP
GW = GH * HD
MESH = pl.DeviceIdType.MESH
F32 = jnp.float32
BF16 = jnp.bfloat16


def remote(src, dst, send, recv, device):
    return pltpu.make_async_remote_copy(
        src_ref=src,
        dst_ref=dst,
        send_sem=send,
        recv_sem=recv,
        device_id={"tile": device},
        device_id_type=MESH,
    )


def place():
    me = lax.axis_index("tile")
    return me, me // GROUP, me % GROUP


def when(cond, body):
    if isinstance(cond, bool):
        if cond:
            body()
    else:
        pl.when(cond)(body)


def stage_blocks(c, cols, s):
    if s == 0:
        return [(c, True, True, True)]
    return [(c - s, c - s >= 0, True, False), (c + s, c + s < cols, False, True)]


def direct_steps(full, cols, zs, zr, ps, pr):
    me, c, p = place()

    def z_copy(d, k):
        to = (c + d) % cols
        return remote(full(k, p), full(k, p), zs(d), zr(d), to * GROUP + p)

    def plane(d, e, q):
        k = (c + cols - d) % cols
        return remote(full(k, q), full(k, q), ps(d, e), pr(d, e), c * GROUP + (p + e) % GROUP)

    for d in range(1, cols):
        z_copy(d, c).start()
    for e in range(1, GROUP):
        plane(0, e, p).start()
    yield
    for d in range(1, cols):
        z_copy(d, (c + cols - d) % cols).wait_recv()
        for e in range(1, GROUP):
            plane(d, e, p).start()
    yield
    for d in range(cols):
        for e in range(1, GROUP):
            plane(d, e, (p + GROUP - e) % GROUP).wait_recv()
    for d in range(cols):
        if d:
            z_copy(d, c).wait_send()
        for e in range(1, GROUP):
            plane(d, e, p).wait_send()


def advance(steps):
    return next(steps, "end") != "end"


def drain(*many):
    live = list(many)
    while live:
        live = [steps for steps in live if advance(steps)]


def embed_kernel(
    cols, x_ref, own_ref, nb_ref, cw_ref, pw_hbm, wq_hbm, wk_hbm, wv_hbm,
    tok_ref, kv_ref, q_ref,
    faces, halo_s, halo_r, nb_all, nb_s, ep, pw, ww,
    n_ss, n_rs, z_ss, z_rs, h_ss, h_rs, local_sem,
):
    me, c, p = place()
    loads = [
        pltpu.make_async_copy(x_ref, ep.at[pl.ds(1, 4), pl.ds(1, 4)], local_sem.at[0]),
        pltpu.make_async_copy(pw_hbm, pw, local_sem.at[1]),
        pltpu.make_async_copy(wq_hbm, ww.at[0], local_sem.at[2]),
        pltpu.make_async_copy(wk_hbm, ww.at[1], local_sem.at[3]),
        pltpu.make_async_copy(wv_hbm, ww.at[2], local_sem.at[4]),
    ]
    barrier = pltpu.get_barrier_semaphore()
    for e in range(1, GROUP):
        pl.semaphore_signal(
            barrier, inc=1, device_id={"tile": c * GROUP + (p + e) % GROUP}, device_id_type=MESH
        )

    @pl.when(c + 1 < cols)
    def _():
        pl.semaphore_signal(barrier, inc=1, device_id={"tile": me + GROUP}, device_id_type=MESH)

    @pl.when(c >= 1)
    def _():
        pl.semaphore_signal(barrier, inc=1, device_id={"tile": me - GROUP}, device_id_type=MESH)

    for load in loads:
        load.start()
    faces[pl.ds(2 * c, 2)] = own_ref[...]
    faces[2 * cols] = jnp.zeros(faces.shape[1:], BF16)
    nb_all[p] = nb_ref[...]
    inner = (c >= 1) & (c + 1 < cols)

    @pl.when(inner)
    def _():
        pl.semaphore_wait(barrier, GROUP + 1)

    @pl.when(jnp.logical_not(inner))
    def _():
        pl.semaphore_wait(barrier, GROUP)

    def n_copy(e):
        return remote(
            nb_all.at[p], nb_all.at[p], n_ss.at[e], n_rs.at[e], c * GROUP + (p + e) % GROUP
        )

    def z_copy(k, way):
        block = faces.at[pl.ds(2 * k, 2)]
        to = c + 1 - 2 * way
        return remote(block, block, z_ss.at[way, k], z_rs.at[k], to * GROUP + p)

    def h_copy(e):
        g = (p + e) % GROUP
        return remote(halo_s.at[g], halo_r.at[p], h_ss.at[e], h_rs.at[e], c * GROUP + g)

    for e in range(1, GROUP):
        n_copy(e).start()
    for s in range(cols):
        for k, ok, up, down in stage_blocks(c, cols, s):
            def body(k=k, up=up, down=down):
                if s > 0:
                    z_copy(k, 0).wait_recv()
                if s < cols - 1:
                    if up:
                        when(c + 1 < cols, lambda: z_copy(k, 0).start())
                    if down:
                        when(c >= 1, lambda: z_copy(k, 1).start())
            when(ok, body)
        if s == 0:
            for e in range(1, GROUP):
                n_copy(e).wait_recv()
            table = pltpu.make_async_copy(nb_all, nb_s, local_sem.at[5])
            table.start()
            table.wait()

    side, ch = faces.shape[2], faces.shape[3]
    tile_dev = 2 * GROUP

    def fill(g, target):
        for t in range(2):
            def face(link, which):
                index = nb_s[g, t, link]
                found = faces[index // tile_dev * 2 + index % 2, which]
                mine = index // 2 % GROUP == p
                return jnp.where(mine, found.astype(F32), 0.0)

            for at, (link, which) in enumerate(((1, 1), (6, 0), (3, 3), (4, 2))):
                target[t, at * side:(at + 1) * side] = face(link, which).astype(BF16)
            corners = jnp.concatenate(
                [
                    face(0, 1)[side - 1:side], face(2, 1)[0:1],
                    face(5, 0)[side - 1:side], face(7, 0)[0:1],
                    jnp.zeros((12, ch), F32),
                ],
                axis=0,
            )
            target[t, 4 * side:4 * side + 16] = corners.astype(BF16)

    for e in range(1, GROUP):
        g = (p + e) % GROUP
        fill(g, halo_s.at[g])
        h_copy(e).start()
    fill(p, halo_r.at[p])

    loads[0].wait()
    first = lax.broadcasted_iota(jnp.int32, (64, ch), 0) % 8

    def spread(col):
        return jnp.broadcast_to(col[:, None, :], (8, 8, ch)).reshape(64, ch)

    for e in range(1, GROUP):
        h_copy(e).wait_recv()
    for t in range(2):
        rows = pl.ds(t * 64, 64)
        halo = halo_r[0, t].astype(F32)
        for g in range(1, GROUP):
            halo = halo + halo_r[g, t].astype(F32)
        upper, lower, left, right = [halo[at * side:(at + 1) * side] for at in range(4)]
        corners = halo[4 * side:4 * side + 8]
        corner_ul, corner_ur = corners[0:1], corners[1:2]
        corner_dl, corner_dr = corners[2:3], corners[3:4]
        for b in range(4):
            part = slice(b * 8, b * 8 + 8)
            above = jnp.concatenate([upper[part], ep[4, b + 1, rows].astype(F32)[0:56]], axis=0)
            below = jnp.concatenate([ep[1, b + 1, rows].astype(F32)[8:64], lower[part]], axis=0)
            ep[0, b + 1, rows] = above.astype(BF16)
            ep[5, b + 1, rows] = below.astype(BF16)
        lefts = [jnp.concatenate([corner_ul, left[24:31]], axis=0)]
        rights = [jnp.concatenate([corner_ur, right[24:31]], axis=0)]
        for a in range(4):
            lefts.append(left[a * 8:a * 8 + 8])
            rights.append(right[a * 8:a * 8 + 8])
        lefts.append(jnp.concatenate([left[1:8], corner_dl], axis=0))
        rights.append(jnp.concatenate([right[1:8], corner_dr], axis=0))
        for a in range(6):
            west = pltpu.roll(ep[a, 4, rows].astype(F32), 1, 0)
            east = pltpu.roll(ep[a, 1, rows].astype(F32), 63, 0)
            ep[a, 0, rows] = jnp.where(first == 0, spread(lefts[a]), west).astype(BF16)
            ep[a, 5, rows] = jnp.where(first == 7, spread(rights[a]), east).astype(BF16)

    loads[1].wait()
    tok = jnp.zeros(tok_ref.shape, F32)
    for i in range(4):
        acc = jnp.zeros((512, ch), F32)
        for dy in range(3):
            for dx in range(3):
                acc = acc + jnp.dot(
                    ep[i + dy, dx:dx + 4].reshape(512, ch), cw_ref[dy * 3 + dx],
                    preferred_element_type=F32,
                )
        hidden = jax.nn.gelu(acc).astype(BF16)
        wide = jnp.concatenate([hidden[j * 128:(j + 1) * 128] for j in range(4)], axis=1)
        tok = tok + jnp.dot(
            wide, pw[i * 4 * ch:(i + 1) * 4 * ch], preferred_element_type=F32
        )
    tokens = tok.astype(BF16)
    tok_ref[...] = tokens
    for load in loads[2:]:
        load.wait()
    query = jnp.dot(tokens, ww[0], preferred_element_type=F32)
    keys = jnp.dot(tokens, ww[1], preferred_element_type=F32)
    values = jnp.dot(tokens, ww[2], preferred_element_type=F32)
    for g in range(GROUP):
        part = slice(g * GW, (g + 1) * GW)
        q_ref[g] = query[:, part].astype(BF16)
        for h in range(GH):
            part = slice(g * GW + h * HD, g * GW + h * HD + HD)
            kv_ref[g, h] = jnp.concatenate([keys[:, part], values[:, part]], axis=1).astype(BF16)
    for e in range(1, GROUP):
        n_copy(e).wait_send()
        h_copy(e).wait_send()
    for s in range(cols - 1):
        for k, ok, up, down in stage_blocks(c, cols, s):
            def body(k=k, up=up, down=down):
                if up:
                    when(c + 1 < cols, lambda: z_copy(k, 0).wait_send())
                if down:
                    when(c >= 1, lambda: z_copy(k, 1).wait_send())
            when(ok, body)


def attend_kernel(
    cols, own_rows, tok_ref, kv_ref, q_ref, cot_ref, wo_ref,
    mixed_ref, grad_ref,
    kvg, qg, og, ogr, cotg, part_f, part_s, part_r, gr,
    kv_ss, kv_rs, q_ss, q_rs, c_ss, c_rs, o_ss, o_rs, z_ss, z_rs, p_ss, p_rs, zs, zr, ss, rs,
):
    n = cols * GROUP
    owners = HD // own_rows
    me, c, p = place()
    barrier = pltpu.get_barrier_semaphore()
    for d in range(1, GROUP):
        pl.semaphore_signal(
            barrier, inc=1, device_id={"tile": c * GROUP + (p + d) % GROUP}, device_id_type=MESH
        )
    for d in range(1, cols):
        pl.semaphore_signal(
            barrier, inc=1, device_id={"tile": (c + d) % cols * GROUP + p}, device_id_type=MESH
        )
    for h in range(GH):
        kvg[h, me] = kv_ref[p, h]
    qg[p] = q_ref[p]
    cotg[p] = cot_ref[...]
    pl.semaphore_wait(barrier, GROUP - 1 + cols - 1)

    def kv_plane(h, d):
        g = (p + d) % GROUP
        return remote(
            kv_ref.at[g, h], kvg.at[h, me], kv_ss.at[h, d], kv_rs.at[h, d], c * GROUP + g
        )

    def q_plane(d):
        g = (p + d) % GROUP
        return remote(q_ref.at[g], qg.at[p], q_ss.at[d], q_rs.at[d], c * GROUP + g)

    def c_plane(d):
        g = (p + d) % GROUP
        return remote(cotg.at[p], cotg.at[p], c_ss.at[d], c_rs.at[d], c * GROUP + g)

    def o_plane(d):
        g = (p + d) % GROUP
        return remote(og.at[g], ogr.at[p], o_ss.at[d], o_rs.at[d], c * GROUP + g)

    def z_copy(h, k, way):
        block = kvg.at[h, pl.ds(k * GROUP, GROUP)]
        to = c + 1 - 2 * way
        return remote(block, block, z_ss.at[h, way, k], z_rs.at[h, k], to * GROUP + p)

    def z_steps(h):
        for d in range(1, GROUP):
            kv_plane(h, d).wait_recv()
        for s in range(cols):
            for k, ok, up, down in stage_blocks(c, cols, s):
                def body(k=k, up=up, down=down):
                    if s > 0:
                        z_copy(h, k, 0).wait_recv()
                    if s < cols - 1:
                        if up:
                            when(c + 1 < cols, lambda: z_copy(h, k, 0).start())
                        if down:
                            when(c >= 1, lambda: z_copy(h, k, 1).start())
                when(ok, body)
            yield

    factor = HD ** (-0.5) * math.log2(math.e)

    def attend(h, first, last):
        lanes = slice(h * HD, (h + 1) * HD)
        count = (last - first) * 128
        both = kvg[h].reshape(n * 128, 2 * HD)
        query = qg[first:last, :, lanes].reshape(count, HD)
        query = jnp.concatenate([query, jnp.zeros_like(query)], axis=1)
        scores = lax.dot_general(
            query, both, (((1,), (1,)), ((), ())), preferred_element_type=F32
        )
        top = jnp.max(scores, axis=1, keepdims=True)
        weights = jnp.exp2((scores - top) * factor)
        total = jnp.sum(weights, axis=1, keepdims=True)
        out = jnp.dot(weights.astype(BF16), both, preferred_element_type=F32)
        out = (out / total)[:, HD:].astype(BF16)
        og[first:last, :, lanes] = out.reshape(last - first, 128, HD)

    def p_copy(h, d):
        j = (c + d) % cols
        return j, remote(
            part_s.at[h, j], part_r.at[h, d], p_ss.at[h, d], p_rs.at[h, d], j * GROUP + p
        )

    def grad_steps(h):
        part = lax.dot_general(
            og[:, :, h * HD:(h + 1) * HD].reshape(GROUP * 128, HD),
            cotg[...].reshape(GROUP * 128, -1),
            (((0,), (0,)), ((), ())), preferred_element_type=F32,
        ).reshape(owners, own_rows, -1)
        part_f[h] = part
        part_s[h] = part.astype(BF16)
        for d in range(1, cols):
            j, copy = p_copy(h, d)
            when(j < owners if owners < cols else True, copy.start)
        yield

        def reduce():
            acc = part_f[h, c]
            for d in range(1, cols):
                p_copy(h, d)[1].wait_recv()
                acc = acc + part_r[h, d].astype(F32)
            gr[h, me] = acc.astype(BF16)

        def nothing():
            gr[h, me] = jnp.zeros(gr.shape[2:], BF16)

        if owners < cols:
            pl.when(c < owners)(reduce)
            pl.when(c >= owners)(nothing)
        else:
            reduce()
        yield from direct_steps(
            lambda k, q: gr.at[h, k * GROUP + q], cols,
            lambda d: zs.at[h, d], lambda d: zr.at[h, d],
            lambda d, e: ss.at[h, d, e], lambda d, e: rs.at[h, d, e],
        )
        for d in range(1, cols):
            j, copy = p_copy(h, d)
            when(j < owners if owners < cols else True, copy.wait_send)

    for h in range(GH):
        for d in range(1, GROUP):
            kv_plane(h, d).start()
    z = [z_steps(h) for h in range(GH)]
    grads = [grad_steps(h) for h in range(GH)]
    advance(z[0])
    advance(z[1])
    advance(z[0])
    advance(z[2])
    for d in range(1, GROUP):
        q_plane(d).start()
    advance(z[0])
    advance(z[1])
    drain(z[0])
    for d in range(1, GROUP):
        q_plane(d).wait_recv()
        c_plane(d).start()
    attend(0, 0, 2)
    advance(z[1])
    advance(z[2])
    attend(0, 2, 4)
    drain(z[1])
    advance(z[2])
    for d in range(1, GROUP):
        c_plane(d).wait_recv()
    advance(grads[0])
    attend(1, 0, 2)
    drain(z[2])
    advance(grads[0])
    attend(1, 2, 4)
    advance(grads[0])
    advance(grads[1])
    attend(2, 0, 2)
    advance(grads[1])
    attend(2, 2, 4)
    for d in range(1, GROUP):
        o_plane(d).start()
    advance(grads[2])
    advance(grads[1])
    ogr[p] = og[p]
    for d in range(1, GROUP):
        o_plane(d).wait_recv()
    total = tok_ref[...].astype(F32)
    for g in range(GROUP):
        total = total + jnp.dot(
            ogr[g], wo_ref[g * GW:(g + 1) * GW], preferred_element_type=F32
        )
    mixed_ref[...] = total.astype(BF16)
    advance(grads[2])
    drain(grads[0], grads[1], grads[2])
    for q in range(GROUP):
        for h in range(GH):
            for k in range(owners):
                row = q * GW + h * HD + k * own_rows
                grad_ref[row:row + own_rows] = gr[h, k * GROUP + q].astype(F32)

    for d in range(1, GROUP):
        for h in range(GH):
            kv_plane(h, d).wait_send()
        q_plane(d).wait_send()
        c_plane(d).wait_send()
        o_plane(d).wait_send()
    for h in range(GH):
        for s in range(cols - 1):
            for k, ok, up, down in stage_blocks(c, cols, s):
                def body(k=k, up=up, down=down):
                    if up:
                        when(c + 1 < cols, lambda: z_copy(h, k, 0).wait_send())
                    if down:
                        when(c >= 1, lambda: z_copy(h, k, 1).wait_send())
                when(ok, body)


def local(
    n, features, neighbours, conv_weight, patch_weight, query_weight, key_weight,
    value_weight, output_weight, cotangent,
):
    cols = n // GROUP
    tiles, side, _, ch = features.shape
    blocks = side // PATCH
    dm = query_weight.shape[0]
    rows = tiles * blocks * blocks
    vmem = pl.BlockSpec(memory_space=pltpu.VMEM)
    anyw = pl.BlockSpec(memory_space=pl.ANY)
    dma = pltpu.SemaphoreType.DMA

    x = features.reshape(tiles, blocks, PATCH, blocks, PATCH, ch).transpose(2, 4, 0, 1, 3, 5)
    own = jnp.stack(
        [
            x[0, :, :, 0].transpose(1, 0, 2, 3),
            x[-1, :, :, -1].transpose(1, 0, 2, 3),
            x[:, 0, :, :, 0].transpose(1, 0, 2, 3),
            x[:, -1, :, :, -1].transpose(1, 0, 2, 3),
        ],
        axis=1,
    ).reshape(tiles, 4, side, ch)
    x = x.reshape(PATCH, PATCH, rows, ch)

    table = jnp.pad(neighbours, ((0, 8 - tiles), (0, 120)))
    tok, kv, q = pl.pallas_call(
        functools.partial(embed_kernel, cols),
        out_shape=(
            jax.ShapeDtypeStruct((rows, dm), BF16),
            jax.ShapeDtypeStruct((GROUP, GH, rows, 2 * HD), BF16),
            jax.ShapeDtypeStruct((GROUP, rows, GW), BF16),
        ),
        in_specs=[anyw, vmem, vmem, vmem, anyw, anyw, anyw, anyw],
        out_specs=(vmem, vmem, vmem),
        scratch_shapes=[
            pltpu.VMEM((2 * cols + 1, 4, side, ch), BF16),
            pltpu.VMEM((GROUP, tiles, 4 * side + 16, ch), BF16),
            pltpu.VMEM((GROUP, tiles, 4 * side + 16, ch), BF16),
            pltpu.VMEM((GROUP, 8, 128), jnp.int32),
            pltpu.SMEM((GROUP, 8, 128), jnp.int32),
            pltpu.VMEM((6, 6, rows, ch), BF16),
            pltpu.VMEM(patch_weight.shape, BF16),
            pltpu.VMEM((3, dm, dm), BF16),
            dma((GROUP,)), dma((GROUP,)),
            dma((2, cols)), dma((cols,)),
            dma((GROUP,)), dma((GROUP,)),
            dma((6,)),
        ],
        compiler_params=pltpu.CompilerParams(
            collective_id=0, has_side_effects=True, vmem_limit_bytes=52 * 2**20
        ),
        name="embed",
    )(
        x, own, table, conv_weight.reshape(9, ch, ch), patch_weight,
        query_weight, key_weight, value_weight,
    )

    own_rows = max(16, HD // cols // 16 * 16)
    owners = HD // own_rows
    mixed, grad = pl.pallas_call(
        functools.partial(attend_kernel, cols, own_rows),
        out_shape=(
            jax.ShapeDtypeStruct((rows, dm), BF16),
            jax.ShapeDtypeStruct((dm, dm), F32),
        ),
        in_specs=[vmem] * 5,
        out_specs=(vmem, vmem),
        scratch_shapes=[
            pltpu.VMEM((GH, n, rows, 2 * HD), BF16),
            pltpu.VMEM((GROUP, rows, GW), BF16),
            pltpu.VMEM((GROUP, rows, GW), BF16),
            pltpu.VMEM((GROUP, rows, GW), BF16),
            pltpu.VMEM((GROUP, rows, dm), BF16),
            pltpu.VMEM((GH, owners, own_rows, dm), F32),
            pltpu.VMEM((GH, owners, own_rows, dm), BF16),
            pltpu.VMEM((GH, cols, own_rows, dm), BF16),
            pltpu.VMEM((GH, n, own_rows, dm), BF16),
            dma((GH, GROUP)), dma((GH, GROUP)),
            dma((GROUP,)), dma((GROUP,)),
            dma((GROUP,)), dma((GROUP,)),
            dma((GROUP,)), dma((GROUP,)),
            dma((GH, 2, cols)), dma((GH, cols)),
            dma((GH, cols)), dma((GH, cols)),
            dma((GH, cols)), dma((GH, cols)),
            dma((GH, cols, GROUP)), dma((GH, cols, GROUP)),
        ],
        compiler_params=pltpu.CompilerParams(
            collective_id=1, has_side_effects=True, vmem_limit_bytes=52 * 2**20
        ),
        name="attend",
    )(tok, kv, q, cotangent, output_weight)
    return mixed, grad


def solution(mesh):
    part = P(("slide", "tile"))
    in_specs = (part, part) + (P(),) * 6 + (part,)
    out_specs = (part, P("slide"))
    return jax.shard_map(
        functools.partial(local, mesh.shape["tile"]),
        mesh=mesh, in_specs=in_specs, out_specs=out_specs, check_vma=False,
    )
```

```python
import functools
import math

import jax
import jax.numpy as jnp
from jax import lax
from jax.experimental import pallas as pl
from jax.experimental.pallas import tpu as pltpu
from jax.sharding import PartitionSpec as P

PATCH = 4
HEADS = 12
HD = 64
GROUP = 4
GH = HEADS // GROUP
GW = GH * HD
MESH = pl.DeviceIdType.MESH
F32 = jnp.float32
BF16 = jnp.bfloat16


def remote(src, dst, send, recv, device):
    return pltpu.make_async_remote_copy(
        src_ref=src,
        dst_ref=dst,
        send_sem=send,
        recv_sem=recv,
        device_id={"tile": device},
        device_id_type=MESH,
    )


def place():
    me = lax.axis_index("tile")
    return me, me // GROUP, me % GROUP


def when(cond, body):
    if isinstance(cond, bool):
        if cond:
            body()
    else:
        pl.when(cond)(body)


def stage_blocks(c, cols, s):
    if s == 0:
        return [(c, True, True, True)]
    return [(c - s, c - s >= 0, True, False), (c + s, c + s < cols, False, True)]


def direct_copies(full, cols, zs, zr, ps, pr):
    me, c, p = place()

    def z_copy(d, k):
        to = (c + d) % cols
        return remote(full(k, p), full(k, p), zs(d), zr(d), to * GROUP + p)

    def plane(d, e, q):
        k = (c + cols - d) % cols
        return remote(full(k, q), full(k, q), ps(d, e), pr(d, e), c * GROUP + (p + e) % GROUP)

    return z_copy, plane


def embed_kernel(
    cols, x_ref, own_ref, nb_ref, cw_ref, pw_hbm, wq_hbm, wk_hbm, wv_hbm,
    tok_ref, kv_ref, q_ref,
    faces, halo_s, halo_r, nb_all, nb_s, ep, pw, ww, tok,
    n_ss, n_rs, z_ss, z_rs, h_ss, h_rs, local_sem,
):
    me, c, p = place()
    loads = [
        pltpu.make_async_copy(x_ref, ep.at[pl.ds(1, 4), pl.ds(1, 4)], local_sem.at[0]),
        pltpu.make_async_copy(pw_hbm, pw, local_sem.at[1]),
        pltpu.make_async_copy(wq_hbm, ww.at[0], local_sem.at[2]),
        pltpu.make_async_copy(wk_hbm, ww.at[1], local_sem.at[3]),
        pltpu.make_async_copy(wv_hbm, ww.at[2], local_sem.at[4]),
    ]
    barrier = pltpu.get_barrier_semaphore()
    for e in range(1, GROUP):
        pl.semaphore_signal(
            barrier, inc=1, device_id={"tile": c * GROUP + (p + e) % GROUP}, device_id_type=MESH
        )

    @pl.when(c + 1 < cols)
    def _():
        pl.semaphore_signal(barrier, inc=1, device_id={"tile": me + GROUP}, device_id_type=MESH)

    @pl.when(c >= 1)
    def _():
        pl.semaphore_signal(barrier, inc=1, device_id={"tile": me - GROUP}, device_id_type=MESH)

    for load in loads:
        load.start()
    faces[pl.ds(2 * c, 2)] = own_ref[...]
    faces[2 * cols] = jnp.zeros(faces.shape[1:], BF16)
    nb_all[p] = nb_ref[...]
    inner = (c >= 1) & (c + 1 < cols)

    @pl.when(inner)
    def _():
        pl.semaphore_wait(barrier, GROUP + 1)

    @pl.when(jnp.logical_not(inner))
    def _():
        pl.semaphore_wait(barrier, GROUP)

    def n_copy(e):
        return remote(
            nb_all.at[p], nb_all.at[p], n_ss.at[e], n_rs.at[e], c * GROUP + (p + e) % GROUP
        )

    def z_copy(k, way):
        block = faces.at[pl.ds(2 * k, 2)]
        to = c + 1 - 2 * way
        return remote(block, block, z_ss.at[way, k], z_rs.at[k], to * GROUP + p)

    def h_copy(e):
        g = (p + e) % GROUP
        return remote(halo_s.at[g], halo_r.at[p], h_ss.at[e], h_rs.at[e], c * GROUP + g)

    for e in range(1, GROUP):
        n_copy(e).start()
    for s in range(cols):
        for k, ok, up, down in stage_blocks(c, cols, s):
            def body(k=k, up=up, down=down):
                if s > 0:
                    z_copy(k, 0).wait_recv()
                if s < cols - 1:
                    if up:
                        when(c + 1 < cols, lambda: z_copy(k, 0).start())
                    if down:
                        when(c >= 1, lambda: z_copy(k, 1).start())
            when(ok, body)
        if s == 0:
            for e in range(1, GROUP):
                n_copy(e).wait_recv()
            table = pltpu.make_async_copy(nb_all, nb_s, local_sem.at[5])
            table.start()
            table.wait()

    side, ch = faces.shape[2], faces.shape[3]
    tile_dev = 2 * GROUP

    def fill(g, target):
        for t in range(2):
            def face(link, which):
                index = nb_s[g, t, link]
                found = faces[index // tile_dev * 2 + index % 2, which]
                mine = index // 2 % GROUP == p
                return jnp.where(mine, found.astype(F32), 0.0)

            for at, (link, which) in enumerate(((1, 1), (6, 0), (3, 3), (4, 2))):
                target[t, at * side:(at + 1) * side] = face(link, which).astype(BF16)
            corners = jnp.concatenate(
                [
                    face(0, 1)[side - 1:side], face(2, 1)[0:1],
                    face(5, 0)[side - 1:side], face(7, 0)[0:1],
                    jnp.zeros((12, ch), F32),
                ],
                axis=0,
            )
            target[t, 4 * side:4 * side + 16] = corners.astype(BF16)

    def fill_send(e, carry):
        g = (p + e) % GROUP
        fill(g, halo_s.at[g])
        h_copy(e).start()
        return carry

    lax.fori_loop(1, GROUP, fill_send, 0)
    fill(p, halo_r.at[p])

    loads[0].wait()
    first = lax.broadcasted_iota(jnp.int32, (64, ch), 0) % 8

    def spread(col):
        return jnp.broadcast_to(col[:, None, :], (8, 8, ch)).reshape(64, ch)

    for e in range(1, GROUP):
        h_copy(e).wait_recv()
    for t in range(2):
        rows = pl.ds(t * 64, 64)
        halo = halo_r[0, t].astype(F32)
        for g in range(1, GROUP):
            halo = halo + halo_r[g, t].astype(F32)
        upper, lower, left, right = [halo[at * side:(at + 1) * side] for at in range(4)]
        corners = halo[4 * side:4 * side + 8]
        corner_ul, corner_ur = corners[0:1], corners[1:2]
        corner_dl, corner_dr = corners[2:3], corners[3:4]
        for b in range(4):
            part = slice(b * 8, b * 8 + 8)
            above = jnp.concatenate([upper[part], ep[4, b + 1, rows].astype(F32)[0:56]], axis=0)
            below = jnp.concatenate([ep[1, b + 1, rows].astype(F32)[8:64], lower[part]], axis=0)
            ep[0, b + 1, rows] = above.astype(BF16)
            ep[5, b + 1, rows] = below.astype(BF16)
        lefts = [jnp.concatenate([corner_ul, left[24:31]], axis=0)]
        rights = [jnp.concatenate([corner_ur, right[24:31]], axis=0)]
        for a in range(4):
            lefts.append(left[a * 8:a * 8 + 8])
            rights.append(right[a * 8:a * 8 + 8])
        lefts.append(jnp.concatenate([left[1:8], corner_dl], axis=0))
        rights.append(jnp.concatenate([right[1:8], corner_dr], axis=0))
        for a in range(6):
            west = pltpu.roll(ep[a, 4, rows].astype(F32), 1, 0)
            east = pltpu.roll(ep[a, 1, rows].astype(F32), 63, 0)
            ep[a, 0, rows] = jnp.where(first == 0, spread(lefts[a]), west).astype(BF16)
            ep[a, 5, rows] = jnp.where(first == 7, spread(rights[a]), east).astype(BF16)

    loads[1].wait()
    tok[...] = jnp.zeros(tok.shape, F32)

    def phase_row(i, carry):
        acc = jnp.zeros((512, ch), F32)
        for dy in range(3):
            for dx in range(3):
                acc = acc + jnp.dot(
                    ep[i + dy, dx:dx + 4].reshape(512, ch), cw_ref[dy * 3 + dx],
                    preferred_element_type=F32,
                )
        hidden = jax.nn.gelu(acc).astype(BF16)
        wide = jnp.concatenate([hidden[j * 128:(j + 1) * 128] for j in range(4)], axis=1)
        tok[...] += jnp.dot(
            wide, pw[pl.ds(pl.multiple_of(i * 4 * ch, 4 * ch), 4 * ch)],
            preferred_element_type=F32,
        )
        return carry

    lax.fori_loop(0, 4, phase_row, 0)
    tokens = tok[...].astype(BF16)
    tok_ref[...] = tokens
    for load in loads[2:]:
        load.wait()
    query = jnp.dot(tokens, ww[0], preferred_element_type=F32)
    keys = jnp.dot(tokens, ww[1], preferred_element_type=F32)
    values = jnp.dot(tokens, ww[2], preferred_element_type=F32)
    for g in range(GROUP):
        for h in range(GH):
            part = slice(g * GW + h * HD, g * GW + h * HD + HD)
            q_ref[g, h] = jnp.concatenate(
                [query[:, part], jnp.zeros((query.shape[0], HD), F32)], axis=1
            ).astype(BF16)
            kv_ref[g, h] = jnp.concatenate([keys[:, part], values[:, part]], axis=1).astype(BF16)
    for e in range(1, GROUP):
        n_copy(e).wait_send()
        h_copy(e).wait_send()
    for s in range(cols - 1):
        for k, ok, up, down in stage_blocks(c, cols, s):
            def body(k=k, up=up, down=down):
                if up:
                    when(c + 1 < cols, lambda: z_copy(k, 0).wait_send())
                if down:
                    when(c >= 1, lambda: z_copy(k, 1).wait_send())
            when(ok, body)


def attend_kernel(
    cols, own_rows, tok_ref, kv_ref, q_ref, cot_ref, wo_ref,
    mixed_ref, grad_ref,
    kvg, qg, og, ogr, cotg, part_f, part_s, part_r, gr, mix,
    kv_ss, kv_rs, q_ss, q_rs, c_ss, c_rs, o_ss, o_rs, z_ss, z_rs, p_ss, p_rs, zs, zr, ss, rs,
):
    n = cols * GROUP
    owners = HD // own_rows
    me, c, p = place()
    barrier = pltpu.get_barrier_semaphore()
    for d in range(1, GROUP):
        pl.semaphore_signal(
            barrier, inc=1, device_id={"tile": c * GROUP + (p + d) % GROUP}, device_id_type=MESH
        )
    for d in range(1, cols):
        pl.semaphore_signal(
            barrier, inc=1, device_id={"tile": (c + d) % cols * GROUP + p}, device_id_type=MESH
        )
    for h in range(GH):
        kvg[h, me] = kv_ref[p, h]
    qg[p] = q_ref[p]
    cotg[p] = cot_ref[...]
    pl.semaphore_wait(barrier, GROUP - 1 + cols - 1)

    def kv_plane(h, d):
        g = (p + d) % GROUP
        return remote(
            kv_ref.at[g, h], kvg.at[h, me], kv_ss.at[h, d], kv_rs.at[h, d], c * GROUP + g
        )

    def q_plane(d):
        g = (p + d) % GROUP
        return remote(q_ref.at[g], qg.at[p], q_ss.at[d], q_rs.at[d], c * GROUP + g)

    def c_plane(d):
        g = (p + d) % GROUP
        return remote(cotg.at[p], cotg.at[p], c_ss.at[d], c_rs.at[d], c * GROUP + g)

    def o_plane(d):
        g = (p + d) % GROUP
        return remote(og.at[g], ogr.at[p], o_ss.at[d], o_rs.at[d], c * GROUP + g)

    def z_copy(h, k, way):
        block = kvg.at[h, pl.ds(k * GROUP, GROUP)]
        to = c + 1 - 2 * way
        return remote(block, block, z_ss.at[h, way, k], z_rs.at[h, k], to * GROUP + p)

    def z_stage(h, s):
        for k, ok, up, down in stage_blocks(c, cols, s):
            def body(k=k, up=up, down=down):
                if s > 0:
                    z_copy(h, k, 0).wait_recv()
                if s < cols - 1:
                    if up:
                        when(c + 1 < cols, lambda: z_copy(h, k, 0).start())
                    if down:
                        when(c >= 1, lambda: z_copy(h, k, 1).start())
            when(ok, body)

    factor = HD ** (-0.5) * math.log2(math.e)

    def attend(h, i):
        both = kvg[h].reshape(n * 128, 2 * HD)
        query = qg[pl.ds(2 * i, 2), h].reshape(256, 2 * HD)
        scores = lax.dot_general(
            query, both, (((1,), (1,)), ((), ())), preferred_element_type=F32
        )
        top = jnp.max(scores, axis=1, keepdims=True)
        weights = jnp.exp2((scores - top) * factor)
        total = jnp.sum(weights, axis=1, keepdims=True)
        out = jnp.dot(weights.astype(BF16), both, preferred_element_type=F32)
        og[pl.ds(2 * i, 2), h] = (out / total).astype(BF16).reshape(2, 128, 2 * HD)

    def p_copy(h, d):
        j = (c + d) % cols
        return j, remote(
            part_s.at[h, j], part_r.at[h, d], p_ss.at[h, d], p_rs.at[h, d], j * GROUP + p
        )

    def partial(h):
        part = lax.dot_general(
            og[:, h].reshape(GROUP * 128, 2 * HD),
            cotg[...].reshape(GROUP * 128, -1),
            (((0,), (0,)), ((), ())), preferred_element_type=F32,
        )[HD:].reshape(owners, own_rows, -1)
        part_f[h] = part
        part_s[h] = part.astype(BF16)
        for d in range(1, cols):
            j, copy = p_copy(h, d)
            when(j < owners if owners < cols else True, copy.start)

    def collect(h):
        def reduce():
            acc = part_f[h, c]
            for d in range(1, cols):
                p_copy(h, d)[1].wait_recv()
                acc = acc + part_r[h, d].astype(F32)
            gr[h, me] = acc.astype(BF16)

        def nothing():
            gr[h, me] = jnp.zeros(gr.shape[2:], BF16)

        if owners < cols:
            pl.when(c < owners)(reduce)
            pl.when(c >= owners)(nothing)
        else:
            reduce()
        g_copies = gather_copies(h)
        for d in range(1, cols):
            g_copies[0](d, c).start()
        for e in range(1, GROUP):
            g_copies[1](0, e, p).start()

    def gather_copies(h):
        return direct_copies(
            lambda k, q: gr.at[h, k * GROUP + q], cols,
            lambda d: zs.at[h, d], lambda d: zr.at[h, d],
            lambda d, e: ss.at[h, d, e], lambda d, e: rs.at[h, d, e],
        )

    def spread_plane(h):
        z_part, plane = gather_copies(h)
        for d in range(1, cols):
            z_part(d, (c + cols - d) % cols).wait_recv()
            for e in range(1, GROUP):
                plane(d, e, p).start()

    def finish(h, carry):
        z_part, plane = gather_copies(h)
        for d in range(cols):
            for e in range(1, GROUP):
                plane(d, e, (p + GROUP - e) % GROUP).wait_recv()
        for d in range(cols):
            if d:
                z_part(d, c).wait_send()
                j, copy = p_copy(h, d)
                when(j < owners if owners < cols else True, copy.wait_send)
            for e in range(1, GROUP):
                plane(d, e, p).wait_send()
        return carry

    for h in range(GH):
        for d in range(1, GROUP):
            kv_plane(h, d).start()
    for d in range(1, GROUP):
        q_plane(d).start()
    for h in range(GH):
        for d in range(1, GROUP):
            kv_plane(h, d).wait_recv()
        z_stage(h, 0)
    for d in range(1, GROUP):
        c_plane(d).start()
    z_stage(0, 1)
    z_stage(0, 2)
    for d in range(1, GROUP):
        q_plane(d).wait_recv()

    def head(h, carry):
        for s in range(3, cols):
            z_stage(h, s)

        @pl.when(h + 1 < GH)
        def _():
            z_stage(h + 1, 1)

        def half(i, inner):
            @pl.when((i == 1) & (h + 1 < GH))
            def _():
                z_stage(h + 1, 2)

            @pl.when((i == 1) & (h >= 1))
            def _():
                collect(h - 1)

            attend(h, i)
            return inner

        lax.fori_loop(0, 2, half, 0)

        @pl.when(h == 0)
        def _():
            for d in range(1, GROUP):
                c_plane(d).wait_recv()

        @pl.when(h == GH - 1)
        def _():
            for d in range(1, GROUP):
                o_plane(d).start()

        partial(h)

        @pl.when(h >= 1)
        def _():
            spread_plane(h - 1)

        return carry

    lax.fori_loop(0, GH, head, 0)
    ogr[p] = og[p]
    for d in range(1, GROUP):
        o_plane(d).wait_recv()
    mix[...] = tok_ref[...].astype(F32)

    def mix_group(g, carry):
        total = mix[...]
        for h in range(GH):
            weight = wo_ref[pl.ds(pl.multiple_of(g * GW + h * HD, HD), HD)]
            total = total + jnp.dot(
                ogr[g, h][:, HD:], weight, preferred_element_type=F32
            )
        mix[...] = total
        return carry

    collect(GH - 1)
    lax.fori_loop(0, GROUP, mix_group, 0)
    mixed_ref[...] = mix[...].astype(BF16)
    spread_plane(GH - 1)
    lax.fori_loop(0, GH, finish, 0)
    for q in range(GROUP):
        for h in range(GH):
            for k in range(owners):
                row = q * GW + h * HD + k * own_rows
                grad_ref[row:row + own_rows] = gr[h, k * GROUP + q].astype(F32)

    for d in range(1, GROUP):
        for h in range(GH):
            kv_plane(h, d).wait_send()
        q_plane(d).wait_send()
        c_plane(d).wait_send()
        o_plane(d).wait_send()
    for h in range(GH):
        for s in range(cols - 1):
            for k, ok, up, down in stage_blocks(c, cols, s):
                def body(k=k, up=up, down=down):
                    if up:
                        when(c + 1 < cols, lambda: z_copy(h, k, 0).wait_send())
                    if down:
                        when(c >= 1, lambda: z_copy(h, k, 1).wait_send())
                when(ok, body)


def local(
    n, features, neighbours, conv_weight, patch_weight, query_weight, key_weight,
    value_weight, output_weight, cotangent,
):
    cols = n // GROUP
    tiles, side, _, ch = features.shape
    blocks = side // PATCH
    dm = query_weight.shape[0]
    rows = tiles * blocks * blocks
    vmem = pl.BlockSpec(memory_space=pltpu.VMEM)
    anyw = pl.BlockSpec(memory_space=pl.ANY)
    dma = pltpu.SemaphoreType.DMA

    x = features.reshape(tiles, blocks, PATCH, blocks, PATCH, ch).transpose(2, 4, 0, 1, 3, 5)
    own = jnp.stack(
        [
            x[0, :, :, 0].transpose(1, 0, 2, 3),
            x[-1, :, :, -1].transpose(1, 0, 2, 3),
            x[:, 0, :, :, 0].transpose(1, 0, 2, 3),
            x[:, -1, :, :, -1].transpose(1, 0, 2, 3),
        ],
        axis=1,
    ).reshape(tiles, 4, side, ch)
    x = x.reshape(PATCH, PATCH, rows, ch)

    table = jnp.pad(neighbours, ((0, 8 - tiles), (0, 120)))
    tok, kv, q = pl.pallas_call(
        functools.partial(embed_kernel, cols),
        out_shape=(
            jax.ShapeDtypeStruct((rows, dm), BF16),
            jax.ShapeDtypeStruct((GROUP, GH, rows, 2 * HD), BF16),
            jax.ShapeDtypeStruct((GROUP, GH, rows, 2 * HD), BF16),
        ),
        in_specs=[anyw, vmem, vmem, vmem, anyw, anyw, anyw, anyw],
        out_specs=(vmem, vmem, vmem),
        scratch_shapes=[
            pltpu.VMEM((2 * cols + 1, 4, side, ch), BF16),
            pltpu.VMEM((GROUP, tiles, 4 * side + 16, ch), BF16),
            pltpu.VMEM((GROUP, tiles, 4 * side + 16, ch), BF16),
            pltpu.VMEM((GROUP, 8, 128), jnp.int32),
            pltpu.SMEM((GROUP, 8, 128), jnp.int32),
            pltpu.VMEM((6, 6, rows, ch), BF16),
            pltpu.VMEM(patch_weight.shape, BF16),
            pltpu.VMEM((3, dm, dm), BF16),
            pltpu.VMEM((rows, dm), F32),
            dma((GROUP,)), dma((GROUP,)),
            dma((2, cols)), dma((cols,)),
            dma((GROUP,)), dma((GROUP,)),
            dma((6,)),
        ],
        compiler_params=pltpu.CompilerParams(
            collective_id=0, has_side_effects=True, vmem_limit_bytes=52 * 2**20
        ),
        name="embed",
    )(
        x, own, table, conv_weight.reshape(9, ch, ch), patch_weight,
        query_weight, key_weight, value_weight,
    )

    own_rows = max(16, HD // cols // 16 * 16)
    owners = HD // own_rows
    mixed, grad = pl.pallas_call(
        functools.partial(attend_kernel, cols, own_rows),
        out_shape=(
            jax.ShapeDtypeStruct((rows, dm), BF16),
            jax.ShapeDtypeStruct((dm, dm), F32),
        ),
        in_specs=[vmem] * 5,
        out_specs=(vmem, vmem),
        scratch_shapes=[
            pltpu.VMEM((GH, n, rows, 2 * HD), BF16),
            pltpu.VMEM((GROUP, GH, rows, 2 * HD), BF16),
            pltpu.VMEM((GROUP, GH, rows, 2 * HD), BF16),
            pltpu.VMEM((GROUP, GH, rows, 2 * HD), BF16),
            pltpu.VMEM((GROUP, rows, dm), BF16),
            pltpu.VMEM((GH, owners, own_rows, dm), F32),
            pltpu.VMEM((GH, owners, own_rows, dm), BF16),
            pltpu.VMEM((GH, cols, own_rows, dm), BF16),
            pltpu.VMEM((GH, n, own_rows, dm), BF16),
            pltpu.VMEM((rows, dm), F32),
            dma((GH, GROUP)), dma((GH, GROUP)),
            dma((GROUP,)), dma((GROUP,)),
            dma((GROUP,)), dma((GROUP,)),
            dma((GROUP,)), dma((GROUP,)),
            dma((GH, 2, cols)), dma((GH, cols)),
            dma((GH, cols)), dma((GH, cols)),
            dma((GH, cols)), dma((GH, cols)),
            dma((GH, cols, GROUP)), dma((GH, cols, GROUP)),
        ],
        compiler_params=pltpu.CompilerParams(
            collective_id=1, has_side_effects=True, vmem_limit_bytes=52 * 2**20
        ),
        name="attend",
    )(tok, kv, q, cotangent, output_weight)
    return mixed, grad


def solution(mesh):
    part = P(("slide", "tile"))
    in_specs = (part, part) + (P(),) * 6 + (part,)
    out_specs = (part, P("slide"))
    return jax.shard_map(
        functools.partial(local, mesh.shape["tile"]),
        mesh=mesh, in_specs=in_specs, out_specs=out_specs, check_vma=False,
    )
```

```python
import functools
import math

import jax
import jax.numpy as jnp
from jax import lax
from jax.experimental import pallas as pl
from jax.experimental.pallas import tpu as pltpu
from jax.sharding import PartitionSpec as P

PATCH = 4
HEADS = 12
HD = 64
GROUP = 4
GH = HEADS // GROUP
GW = GH * HD
MESH = pl.DeviceIdType.MESH
F32 = jnp.float32
BF16 = jnp.bfloat16


def remote(src, dst, send, recv, device):
    return pltpu.make_async_remote_copy(
        src_ref=src,
        dst_ref=dst,
        send_sem=send,
        recv_sem=recv,
        device_id={"tile": device},
        device_id_type=MESH,
    )


def place():
    me = lax.axis_index("tile")
    return me, me // GROUP, me % GROUP


def when(cond, body):
    if isinstance(cond, bool):
        if cond:
            body()
    else:
        pl.when(cond)(body)


def stage_blocks(c, cols, s):
    if s == 0:
        return [(c, True, True, True)]
    return [(c - s, c - s >= 0, True, False), (c + s, c + s < cols, False, True)]


def direct_copies(full, cols, zs, zr, ps, pr):
    me, c, p = place()

    def z_copy(d, k):
        to = (c + d) % cols
        return remote(full(k, p), full(k, p), zs(d), zr(d), to * GROUP + p)

    def plane(d, e, q):
        k = (c + cols - d) % cols
        return remote(full(k, q), full(k, q), ps(d, e), pr(d, e), c * GROUP + (p + e) % GROUP)

    return z_copy, plane


def embed_kernel(
    cols, x_ref, own_ref, nb_ref, cw_ref, pw_hbm, wq_hbm, wk_hbm, wv_hbm,
    tok_ref, kv_ref, q_ref,
    faces, halo_s, halo_r, nb_all, nb_s, ep, pw, ww, tok,
    n_ss, n_rs, z_ss, z_rs, h_ss, h_rs, local_sem,
):
    me, c, p = place()
    loads = [
        pltpu.make_async_copy(x_ref, ep.at[pl.ds(1, 4), pl.ds(1, 4)], local_sem.at[0]),
        pltpu.make_async_copy(pw_hbm, pw, local_sem.at[1]),
        pltpu.make_async_copy(wq_hbm, ww.at[0], local_sem.at[2]),
        pltpu.make_async_copy(wk_hbm, ww.at[1], local_sem.at[3]),
        pltpu.make_async_copy(wv_hbm, ww.at[2], local_sem.at[4]),
    ]
    barrier = pltpu.get_barrier_semaphore()
    for e in range(1, GROUP):
        pl.semaphore_signal(
            barrier, inc=1, device_id={"tile": c * GROUP + (p + e) % GROUP}, device_id_type=MESH
        )

    @pl.when(c + 1 < cols)
    def _():
        pl.semaphore_signal(barrier, inc=1, device_id={"tile": me + GROUP}, device_id_type=MESH)

    @pl.when(c >= 1)
    def _():
        pl.semaphore_signal(barrier, inc=1, device_id={"tile": me - GROUP}, device_id_type=MESH)

    for load in loads:
        load.start()
    faces[pl.ds(2 * c, 2)] = own_ref[...]
    faces[2 * cols] = jnp.zeros(faces.shape[1:], BF16)
    nb_all[p] = jnp.zeros(nb_all.shape[1:], jnp.int32)
    nb_all[p, 0:nb_ref.shape[0], 0:nb_ref.shape[1]] = nb_ref[...]
    inner = (c >= 1) & (c + 1 < cols)

    @pl.when(inner)
    def _():
        pl.semaphore_wait(barrier, GROUP + 1)

    @pl.when(jnp.logical_not(inner))
    def _():
        pl.semaphore_wait(barrier, GROUP)

    def n_copy(e):
        return remote(
            nb_all.at[p], nb_all.at[p], n_ss.at[e], n_rs.at[e], c * GROUP + (p + e) % GROUP
        )

    def z_copy(k, way):
        block = faces.at[pl.ds(2 * k, 2)]
        to = c + 1 - 2 * way
        return remote(block, block, z_ss.at[way, k], z_rs.at[k], to * GROUP + p)

    def h_copy(e):
        g = (p + e) % GROUP
        return remote(halo_s.at[g], halo_r.at[p], h_ss.at[e], h_rs.at[e], c * GROUP + g)

    for e in range(1, GROUP):
        n_copy(e).start()
    for s in range(cols):
        for k, ok, up, down in stage_blocks(c, cols, s):
            def body(k=k, up=up, down=down):
                if s > 0:
                    z_copy(k, 0).wait_recv()
                if s < cols - 1:
                    if up:
                        when(c + 1 < cols, lambda: z_copy(k, 0).start())
                    if down:
                        when(c >= 1, lambda: z_copy(k, 1).start())
            when(ok, body)
        if s == 0:
            for e in range(1, GROUP):
                n_copy(e).wait_recv()
            table = pltpu.make_async_copy(nb_all, nb_s, local_sem.at[5])
            table.start()
            table.wait()

    side, ch = faces.shape[2], faces.shape[3]
    tile_dev = 2 * GROUP

    def fill(g, target):
        for t in range(2):
            def face(link, which):
                index = nb_s[g, t, link]
                found = faces[index // tile_dev * 2 + index % 2, which]
                mine = index // 2 % GROUP == p
                return jnp.where(mine, found.astype(F32), 0.0)

            for at, (link, which) in enumerate(((1, 1), (6, 0), (3, 3), (4, 2))):
                target[t, at * side:(at + 1) * side] = face(link, which).astype(BF16)
            corners = jnp.concatenate(
                [
                    face(0, 1)[side - 1:side], face(2, 1)[0:1],
                    face(5, 0)[side - 1:side], face(7, 0)[0:1],
                    jnp.zeros((12, ch), F32),
                ],
                axis=0,
            )
            target[t, 4 * side:4 * side + 16] = corners.astype(BF16)

    def fill_send(e, carry):
        g = (p + e) % GROUP
        fill(g, halo_s.at[g])
        h_copy(e).start()
        return carry

    lax.fori_loop(1, GROUP, fill_send, 0)
    fill(p, halo_r.at[p])

    loads[0].wait()
    first = lax.broadcasted_iota(jnp.int32, (64, ch), 0) % 8

    def spread(col):
        return jnp.broadcast_to(col[:, None, :], (8, 8, ch)).reshape(64, ch)

    for e in range(1, GROUP):
        h_copy(e).wait_recv()
    for t in range(2):
        rows = pl.ds(t * 64, 64)
        halo = halo_r[0, t].astype(F32)
        for g in range(1, GROUP):
            halo = halo + halo_r[g, t].astype(F32)
        upper, lower, left, right = [halo[at * side:(at + 1) * side] for at in range(4)]
        corners = halo[4 * side:4 * side + 8]
        corner_ul, corner_ur = corners[0:1], corners[1:2]
        corner_dl, corner_dr = corners[2:3], corners[3:4]
        for b in range(4):
            part = slice(b * 8, b * 8 + 8)
            above = jnp.concatenate([upper[part], ep[4, b + 1, rows].astype(F32)[0:56]], axis=0)
            below = jnp.concatenate([ep[1, b + 1, rows].astype(F32)[8:64], lower[part]], axis=0)
            ep[0, b + 1, rows] = above.astype(BF16)
            ep[5, b + 1, rows] = below.astype(BF16)
        lefts = [jnp.concatenate([corner_ul, left[24:31]], axis=0)]
        rights = [jnp.concatenate([corner_ur, right[24:31]], axis=0)]
        for a in range(4):
            lefts.append(left[a * 8:a * 8 + 8])
            rights.append(right[a * 8:a * 8 + 8])
        lefts.append(jnp.concatenate([left[1:8], corner_dl], axis=0))
        rights.append(jnp.concatenate([right[1:8], corner_dr], axis=0))
        for a in range(6):
            west = pltpu.roll(ep[a, 4, rows].astype(F32), 1, 0)
            east = pltpu.roll(ep[a, 1, rows].astype(F32), 63, 0)
            ep[a, 0, rows] = jnp.where(first == 0, spread(lefts[a]), west).astype(BF16)
            ep[a, 5, rows] = jnp.where(first == 7, spread(rights[a]), east).astype(BF16)

    loads[1].wait()
    tok[...] = jnp.zeros(tok.shape, F32)

    def phase_row(i, carry):
        acc = jnp.zeros((512, ch), F32)
        for dy in range(3):
            for dx in range(3):
                acc = acc + jnp.dot(
                    ep[i + dy, dx:dx + 4].reshape(512, ch), cw_ref[dy * 3 + dx],
                    preferred_element_type=F32,
                )
        hidden = jax.nn.gelu(acc).astype(BF16)
        wide = jnp.concatenate([hidden[j * 128:(j + 1) * 128] for j in range(4)], axis=1)
        tok[...] += jnp.dot(
            wide, pw[pl.ds(pl.multiple_of(i * 4 * ch, 4 * ch), 4 * ch)],
            preferred_element_type=F32,
        )
        return carry

    lax.fori_loop(0, 4, phase_row, 0)
    tokens = tok[...].astype(BF16)
    tok_ref[...] = tokens
    for load in loads[2:]:
        load.wait()
    query = jnp.dot(tokens, ww[0], preferred_element_type=F32)
    keys = jnp.dot(tokens, ww[1], preferred_element_type=F32)
    values = jnp.dot(tokens, ww[2], preferred_element_type=F32)
    for g in range(GROUP):
        for h in range(GH):
            part = slice(g * GW + h * HD, g * GW + h * HD + HD)
            q_ref[g, h] = jnp.concatenate(
                [query[:, part], jnp.zeros((query.shape[0], HD), F32)], axis=1
            ).astype(BF16)
            kv_ref[g, h] = jnp.concatenate([keys[:, part], values[:, part]], axis=1).astype(BF16)
    for e in range(1, GROUP):
        n_copy(e).wait_send()
        h_copy(e).wait_send()
    for s in range(cols - 1):
        for k, ok, up, down in stage_blocks(c, cols, s):
            def body(k=k, up=up, down=down):
                if up:
                    when(c + 1 < cols, lambda: z_copy(k, 0).wait_send())
                if down:
                    when(c >= 1, lambda: z_copy(k, 1).wait_send())
            when(ok, body)


def attend_kernel(
    cols, own_rows, tok_ref, kv_ref, q_ref, cot_ref, wo_ref,
    mixed_ref, grad_ref,
    kvg, qg, og, ogr, cotg, part_f, part_s, part_r, gr, mix,
    kv_ss, kv_rs, q_ss, q_rs, c_ss, c_rs, o_ss, o_rs, z_ss, z_rs, p_ss, p_rs, zs, zr, ss, rs,
):
    n = cols * GROUP
    owners = HD // own_rows
    me, c, p = place()
    barrier = pltpu.get_barrier_semaphore()
    for d in range(1, GROUP):
        pl.semaphore_signal(
            barrier, inc=1, device_id={"tile": c * GROUP + (p + d) % GROUP}, device_id_type=MESH
        )
    for d in range(1, cols):
        pl.semaphore_signal(
            barrier, inc=1, device_id={"tile": (c + d) % cols * GROUP + p}, device_id_type=MESH
        )
    for h in range(GH):
        kvg[h, me] = kv_ref[p, h]
    qg[p] = q_ref[p]
    cotg[p] = cot_ref[...]
    pl.semaphore_wait(barrier, GROUP - 1 + cols - 1)

    def kv_plane(h, d):
        g = (p + d) % GROUP
        return remote(
            kv_ref.at[g, h], kvg.at[h, me], kv_ss.at[h, d], kv_rs.at[h, d], c * GROUP + g
        )

    def q_plane(d):
        g = (p + d) % GROUP
        return remote(q_ref.at[g], qg.at[p], q_ss.at[d], q_rs.at[d], c * GROUP + g)

    def c_plane(d):
        g = (p + d) % GROUP
        return remote(cotg.at[p], cotg.at[p], c_ss.at[d], c_rs.at[d], c * GROUP + g)

    def o_plane(d):
        g = (p + d) % GROUP
        return remote(og.at[g], ogr.at[p], o_ss.at[d], o_rs.at[d], c * GROUP + g)

    def z_copy(h, k, way):
        block = kvg.at[h, pl.ds(k * GROUP, GROUP)]
        to = c + 1 - 2 * way
        return remote(block, block, z_ss.at[h, way, k], z_rs.at[h, k], to * GROUP + p)

    def z_stage(h, s):
        for k, ok, up, down in stage_blocks(c, cols, s):
            def body(k=k, up=up, down=down):
                if s > 0:
                    z_copy(h, k, 0).wait_recv()
                if s < cols - 1:
                    if up:
                        when(c + 1 < cols, lambda: z_copy(h, k, 0).start())
                    if down:
                        when(c >= 1, lambda: z_copy(h, k, 1).start())
            when(ok, body)

    factor = HD ** (-0.5) * math.log2(math.e)

    def attend(h, i):
        both = kvg[h].reshape(n * 128, 2 * HD)
        query = qg[pl.ds(2 * i, 2), h].reshape(256, 2 * HD)
        scores = lax.dot_general(
            query, both, (((1,), (1,)), ((), ())), preferred_element_type=F32
        )
        top = jnp.max(scores, axis=1, keepdims=True)
        weights = jnp.exp2((scores - top) * factor)
        total = jnp.sum(weights, axis=1, keepdims=True)
        out = jnp.dot(weights.astype(BF16), both, preferred_element_type=F32)
        og[pl.ds(2 * i, 2), h] = (out / total).astype(BF16).reshape(2, 128, 2 * HD)

    def p_copy(h, d):
        j = (c + d) % cols
        return j, remote(
            part_s.at[h, j], part_r.at[h, d], p_ss.at[h, d], p_rs.at[h, d], j * GROUP + p
        )

    def partial(h):
        part = lax.dot_general(
            og[:, h].reshape(GROUP * 128, 2 * HD),
            cotg[...].reshape(GROUP * 128, -1),
            (((0,), (0,)), ((), ())), preferred_element_type=F32,
        )[HD:].reshape(owners, own_rows, -1)
        part_f[h] = part
        part_s[h] = part.astype(BF16)
        for d in range(1, cols):
            j, copy = p_copy(h, d)
            when(j < owners if owners < cols else True, copy.start)

    def collect(h):
        def reduce():
            acc = part_f[h, c]
            for d in range(1, cols):
                p_copy(h, d)[1].wait_recv()
                acc = acc + part_r[h, d].astype(F32)
            gr[h, me] = acc.astype(BF16)

        def nothing():
            gr[h, me] = jnp.zeros(gr.shape[2:], BF16)

        if owners < cols:
            pl.when(c < owners)(reduce)
            pl.when(c >= owners)(nothing)
        else:
            reduce()
        g_copies = gather_copies(h)
        for d in range(1, cols):
            g_copies[0](d, c).start()
        for e in range(1, GROUP):
            g_copies[1](0, e, p).start()

    def gather_copies(h):
        return direct_copies(
            lambda k, q: gr.at[h, k * GROUP + q], cols,
            lambda d: zs.at[h, d], lambda d: zr.at[h, d],
            lambda d, e: ss.at[h, d, e], lambda d, e: rs.at[h, d, e],
        )

    def spread_plane(h):
        z_part, plane = gather_copies(h)
        for d in range(1, cols):
            z_part(d, (c + cols - d) % cols).wait_recv()
            for e in range(1, GROUP):
                plane(d, e, p).start()

    def finish(h, carry):
        z_part, plane = gather_copies(h)
        for d in range(cols):
            for e in range(1, GROUP):
                plane(d, e, (p + GROUP - e) % GROUP).wait_recv()
        for d in range(cols):
            if d:
                z_part(d, c).wait_send()
                j, copy = p_copy(h, d)
                when(j < owners if owners < cols else True, copy.wait_send)
            for e in range(1, GROUP):
                plane(d, e, p).wait_send()
        return carry

    for h in range(GH):
        for d in range(1, GROUP):
            kv_plane(h, d).start()
    for d in range(1, GROUP):
        q_plane(d).start()
    for h in range(GH):
        for d in range(1, GROUP):
            kv_plane(h, d).wait_recv()
        z_stage(h, 0)
    for d in range(1, GROUP):
        c_plane(d).start()
    z_stage(0, 1)
    z_stage(0, 2)
    for d in range(1, GROUP):
        q_plane(d).wait_recv()

    def head(h, carry):
        for s in range(3, cols):
            z_stage(h, s)

        @pl.when(h + 1 < GH)
        def _():
            z_stage(h + 1, 1)

        def half(i, inner):
            @pl.when((i == 1) & (h + 1 < GH))
            def _():
                z_stage(h + 1, 2)

            @pl.when((i == 1) & (h >= 1))
            def _():
                collect(h - 1)

            attend(h, i)
            return inner

        lax.fori_loop(0, 2, half, 0)

        @pl.when(h == 0)
        def _():
            for d in range(1, GROUP):
                c_plane(d).wait_recv()

        @pl.when(h == GH - 1)
        def _():
            for d in range(1, GROUP):
                o_plane(d).start()

        partial(h)

        @pl.when(h >= 1)
        def _():
            spread_plane(h - 1)

        return carry

    lax.fori_loop(0, GH, head, 0)
    ogr[p] = og[p]
    for d in range(1, GROUP):
        o_plane(d).wait_recv()
    mix[...] = tok_ref[...].astype(F32)

    def mix_group(g, carry):
        total = mix[...]
        for h in range(GH):
            weight = wo_ref[pl.ds(pl.multiple_of(g * GW + h * HD, HD), HD)]
            total = total + jnp.dot(
                ogr[g, h][:, HD:], weight, preferred_element_type=F32
            )
        mix[...] = total
        return carry

    collect(GH - 1)
    lax.fori_loop(0, GROUP, mix_group, 0)
    mixed_ref[...] = mix[...].astype(BF16)
    spread_plane(GH - 1)
    lax.fori_loop(0, GH, finish, 0)
    for q in range(GROUP):
        for h in range(GH):
            for k in range(owners):
                row = q * GW + h * HD + k * own_rows
                grad_ref[row:row + own_rows] = gr[h, k * GROUP + q]

    for d in range(1, GROUP):
        for h in range(GH):
            kv_plane(h, d).wait_send()
        q_plane(d).wait_send()
        c_plane(d).wait_send()
        o_plane(d).wait_send()
    for h in range(GH):
        for s in range(cols - 1):
            for k, ok, up, down in stage_blocks(c, cols, s):
                def body(k=k, up=up, down=down):
                    if up:
                        when(c + 1 < cols, lambda: z_copy(h, k, 0).wait_send())
                    if down:
                        when(c >= 1, lambda: z_copy(h, k, 1).wait_send())
                when(ok, body)


def widen_kernel(mixed_ref, grad_ref, mixed_out, grad_out):
    mixed_out[...] = mixed_ref[...]
    grad_out[...] = grad_ref[...].astype(F32)


def local(
    n, features, neighbours, conv_weight, patch_weight, query_weight, key_weight,
    value_weight, output_weight, cotangent,
):
    cols = n // GROUP
    tiles, side, _, ch = features.shape
    blocks = side // PATCH
    dm = query_weight.shape[0]
    rows = tiles * blocks * blocks
    vmem = pl.BlockSpec(memory_space=pltpu.VMEM)
    anyw = pl.BlockSpec(memory_space=pl.ANY)
    dma = pltpu.SemaphoreType.DMA

    x = features.reshape(tiles, blocks, PATCH, blocks, PATCH, ch).transpose(2, 4, 0, 1, 3, 5)
    own = jnp.stack(
        [
            x[0, :, :, 0].transpose(1, 0, 2, 3),
            x[-1, :, :, -1].transpose(1, 0, 2, 3),
            x[:, 0, :, :, 0].transpose(1, 0, 2, 3),
            x[:, -1, :, :, -1].transpose(1, 0, 2, 3),
        ],
        axis=1,
    ).reshape(tiles, 4, side, ch)
    x = x.reshape(PATCH, PATCH, rows, ch)

    tok, kv, q = pl.pallas_call(
        functools.partial(embed_kernel, cols),
        out_shape=(
            jax.ShapeDtypeStruct((rows, dm), BF16),
            jax.ShapeDtypeStruct((GROUP, GH, rows, 2 * HD), BF16),
            jax.ShapeDtypeStruct((GROUP, GH, rows, 2 * HD), BF16),
        ),
        in_specs=[anyw, vmem, vmem, vmem, anyw, anyw, anyw, anyw],
        out_specs=(vmem, vmem, vmem),
        scratch_shapes=[
            pltpu.VMEM((2 * cols + 1, 4, side, ch), BF16),
            pltpu.VMEM((GROUP, tiles, 4 * side + 16, ch), BF16),
            pltpu.VMEM((GROUP, tiles, 4 * side + 16, ch), BF16),
            pltpu.VMEM((GROUP, 8, 128), jnp.int32),
            pltpu.SMEM((GROUP, 8, 128), jnp.int32),
            pltpu.VMEM((6, 6, rows, ch), BF16),
            pltpu.VMEM(patch_weight.shape, BF16),
            pltpu.VMEM((3, dm, dm), BF16),
            pltpu.VMEM((rows, dm), F32),
            dma((GROUP,)), dma((GROUP,)),
            dma((2, cols)), dma((cols,)),
            dma((GROUP,)), dma((GROUP,)),
            dma((6,)),
        ],
        compiler_params=pltpu.CompilerParams(
            collective_id=0, has_side_effects=True, vmem_limit_bytes=52 * 2**20
        ),
        name="embed",
    )(
        x, own, neighbours, conv_weight.reshape(9, ch, ch), patch_weight,
        query_weight, key_weight, value_weight,
    )

    own_rows = max(16, HD // cols // 16 * 16)
    owners = HD // own_rows
    mixed, grad = pl.pallas_call(
        functools.partial(attend_kernel, cols, own_rows),
        out_shape=(
            jax.ShapeDtypeStruct((rows, dm), BF16),
            jax.ShapeDtypeStruct((dm, dm), BF16),
        ),
        in_specs=[vmem] * 5,
        out_specs=(vmem, vmem),
        scratch_shapes=[
            pltpu.VMEM((GH, n, rows, 2 * HD), BF16),
            pltpu.VMEM((GROUP, GH, rows, 2 * HD), BF16),
            pltpu.VMEM((GROUP, GH, rows, 2 * HD), BF16),
            pltpu.VMEM((GROUP, GH, rows, 2 * HD), BF16),
            pltpu.VMEM((GROUP, rows, dm), BF16),
            pltpu.VMEM((GH, owners, own_rows, dm), F32),
            pltpu.VMEM((GH, owners, own_rows, dm), BF16),
            pltpu.VMEM((GH, cols, own_rows, dm), BF16),
            pltpu.VMEM((GH, n, own_rows, dm), BF16),
            pltpu.VMEM((rows, dm), F32),
            dma((GH, GROUP)), dma((GH, GROUP)),
            dma((GROUP,)), dma((GROUP,)),
            dma((GROUP,)), dma((GROUP,)),
            dma((GROUP,)), dma((GROUP,)),
            dma((GH, 2, cols)), dma((GH, cols)),
            dma((GH, cols)), dma((GH, cols)),
            dma((GH, cols)), dma((GH, cols)),
            dma((GH, cols, GROUP)), dma((GH, cols, GROUP)),
        ],
        compiler_params=pltpu.CompilerParams(
            collective_id=1, has_side_effects=True, vmem_limit_bytes=52 * 2**20
        ),
        name="attend",
    )(tok, kv, q, cotangent, output_weight)
    whole = pl.BlockSpec((rows, dm), lambda i: (0, 0))
    third = pl.BlockSpec((dm // 3, dm), lambda i: (i, 0))
    return pl.pallas_call(
        widen_kernel,
        grid=(3,),
        out_shape=(
            jax.ShapeDtypeStruct((rows, dm), BF16),
            jax.ShapeDtypeStruct((dm, dm), F32),
        ),
        in_specs=[whole, third],
        out_specs=(whole, third),
        name="widen",
    )(mixed, grad)


def solution(mesh):
    part = P(("slide", "tile"))
    in_specs = (part, part) + (P(),) * 6 + (part,)
    out_specs = (part, P("slide"))
    return jax.shard_map(
        functools.partial(local, mesh.shape["tile"]),
        mesh=mesh, in_specs=in_specs, out_specs=out_specs, check_vma=False,
    )
```
